128 devices in a mesh: pool: 2 (over core), grp: 16 (over z, x), tp: 4 (over y).
Axes of the slice: x: 4, y: 4, z: 4, core: 2. Of those that a mesh axis runs over, the one named last changes fastest.
Arguments:
- queries: bfloat16 [1024, 6144], P(('pool', 'grp'), 'tp'), may hold values from -20 to 20
- key_cache: bfloat16 [1024, 128, 1024], P(('pool', 'grp'), None, 'tp'), may hold values from -20 to 20
- value_cache: bfloat16 [1024, 128, 1024], P(('pool', 'grp'), None, 'tp'), may hold values from -6 to 6
- key_new: bfloat16 [1024, 1024], P(('pool', 'grp'), 'tp'), may hold values from -6 to 6
- value_new: bfloat16 [1024, 1024], P(('pool', 'grp'), 'tp'), may hold values from -6 to 6
- lengths: int32 [1024], P(('pool', 'grp')), may hold values from 2 to 128
- residual: bfloat16 [1024, 6144], P(('pool', 'grp'), 'tp'), may hold values from -6 to 6
- norm_gain: bfloat16 [6144], P('tp'), may hold values from 0.099609375 to 1.8984375
- w_router: bfloat16 [6144, 8], P('tp'), may hold values from -0.078125 to 0.078125
- expert_ids: int32 [1024, 2], P(('pool', 'grp')), may hold values from 0 to 7, all different within a row; in each aligned block of 32 rows (0 to 31, 32 to 63, ...) at most 16 rows name the same one
- w_gate: bfloat16 [6144, 65536], P(None, ('pool', 'grp', 'tp')), may hold values from -0.078125 to 0.078125
- w_up: bfloat16 [6144, 65536], P(None, ('pool', 'grp', 'tp')), may hold values from -0.078125 to 0.078125
- w_down: bfloat16 [65536, 6144], P(('pool', 'grp', 'tp')), may hold values from -0.0625 to 0.0625
Outputs:
- layer_out: bfloat16 [1024, 6144], P(('pool', 'grp'), 'tp')
The draws below stay inside these ranges and needn't reach their ends.
Inputs may be any that keep to these rules, and one draw needn't show every extreme that they name: `expert_ids`: each row names 2 different experts. In each aligned block of 32 rows (the rows of one device) no expert is named by more than 16 rows.
All inputs are finite; a program needn't handle non-finite values.
Results may differ from the reference program's by a relative error of at most 0.0065.
Values may be sent and summed in bfloat16 or wider, within the bound.
No kernel may reach another device: no remote copies, remote signals or barrier semaphores. Data moves between devices by JAX's collectives and lax.ppermute only.
A program may use at most 128 MiB of HBM per device.

```python
import math
import jax
import jax.numpy as jnp
import numpy as np
from jax import lax

D = 6144
HEADS = 48
KVH = 8
HD = 128
EXPERTS = 8
TOP = 2
FF_WIN = 8192
CACHE = 128
REQ_DEV = 32
CAP = 16
REQUESTS = 1024


def draw_queries(key, part):
    key = jax.random.fold_in(key, 1)
    values = jax.random.truncated_normal(key, -4.0, 4.0, (REQUESTS, HEADS * HD), jnp.float32)
    return values.astype(jnp.bfloat16)


def draw_key_cache(key, part):
    key = jax.random.fold_in(key, 2)
    values = jax.random.truncated_normal(key, -4.0, 4.0, (REQUESTS, CACHE, KVH * HD), jnp.float32)
    return values.astype(jnp.bfloat16)


def draw_lengths(key, part):
    key = jax.random.fold_in(key, 3)
    values = jax.random.randint(key, (REQUESTS,), 2, CACHE + 1, jnp.int32)
    return values.at[0].set(CACHE)


def block_scale(stream_key, shape, shards, least, top_value):
    gain, own = 1.0, jax.random.fold_in(stream_key, 6)
    for dim, parts in shards:
        draws = jnp.exp(jax.random.uniform(jax.random.fold_in(own, dim), (parts,), jnp.float32, least / len(shards), top_value / len(shards)))
        gain = gain * jnp.repeat(draws, shape[dim] // parts).reshape([-1 if axis == dim else 1 for axis in range(len(shape))])
    return gain


def shared_out(own_key, own, number, rows, number_of, top, limit, skew):
    ranking = jax.random.permutation(own_key, number_of)
    crowded, ordinary = load_shares(number_of, rows * top, limit, skew, True), load_shares(number_of, rows * top, limit, skew, False)
    places = jnp.arange(number_of)

    def named(sizes, offset_by):
        used = int((sizes > 0).sum())
        fixed = max(1, used // 4)
        passed = fixed + (places - fixed + offset_by * (used - fixed)) % max(1, number_of - fixed)
        return jnp.zeros((number_of,), jnp.int32).at[ranking[jnp.where(places < fixed, places, passed)]].set(jnp.asarray(sizes, jnp.int32))

    sizes = jnp.where(number % 4 == 0, named(crowded, number // 4), named(ordinary, number - number // 4 - 1))
    mixed = jax.random.permutation(jax.random.fold_in(own, 3), number_of)
    donor, receiver = mixed[0:number_of // 2 * 2:2], mixed[1:number_of // 2 * 2:2]
    margin = jnp.minimum(sizes[donor] - 1, limit - sizes[receiver]) // 2
    margin = jnp.where((donor == ranking[0]) | (receiver == ranking[0]) | (sizes[receiver] == 0), 0, jnp.maximum(margin, 0))
    passed = jax.random.randint(jax.random.fold_in(own, 4), (number_of // 2,), 0, 1 << 20) % (margin + 1)
    sizes = sizes.at[donor].add(-passed).at[receiver].add(passed)
    items = jnp.searchsorted(jnp.cumsum(sizes), jnp.arange(rows * top), side="right").astype(jnp.int32)
    table = items.reshape(top, rows).T
    table = table[jax.random.permutation(jax.random.fold_in(own, 1), rows)]
    offset_by = jax.random.randint(jax.random.fold_in(own, 2), (rows, 1), 0, top)
    return jnp.take_along_axis(table, (jnp.arange(top)[None, :] + offset_by) % top, axis=1)


def load_shares(number_of, total, bound, slope, full):
    weights = [(1 << 20) // math.isqrt(standing ** slope) + 1 for standing in range(1, number_of + 1)]
    largest = bound if full else min(bound, max(-(-total // number_of), total * weights[0] // sum(weights)))
    least = 1 if total - largest >= number_of - 1 else 0
    given, spare = [largest] + [least] * (number_of - 1), total - largest - least * (number_of - 1)
    while spare > 0:
        candidates = [i for i in range(1, number_of) if given[i] < largest] or [i for i in range(1, number_of) if given[i] < bound]
        whole, remaining = sum([weights[i] for i in candidates]), spare
        for i in candidates:
            addition = min(bound - given[i], max(1, remaining * weights[i] // whole), spare)
            given[i] = given[i] + addition
            spare = spare - addition
    return np.array(given)


def scatter_about(key, extent, scale, bound, pieces=(), kind=jnp.bfloat16):
    array = jax.random.normal(key, extent, jnp.float32) * scale
    if len(pieces) > 0:
        array = block_scale(key, extent, pieces, -0.22, 0.18) * array
    return jnp.clip(array, min=-bound, max=bound).astype(kind)


def setup_inputs(seed: int = 0) -> dict:
    key_of = jax.random.split(jax.random.key(seed), 14)
    queries = draw_queries(jax.random.fold_in(key_of[13], 71), 0)
    key_cache = draw_key_cache(jax.random.fold_in(key_of[13], 71), 0)
    value_cache = scatter_about(key_of[2], (REQUESTS, CACHE, KVH * HD), 1.0, 6.0, ((0, 32), (2, 4)))
    key_new = scatter_about(key_of[3], (REQUESTS, KVH * HD), 1.0, 6.0, ((0, 32), (1, 4)))
    value_new = scatter_about(key_of[4], (REQUESTS, KVH * HD), 1.0, 6.0, ((0, 32), (1, 4)))
    lengths = draw_lengths(jax.random.fold_in(key_of[13], 71), 0)
    residual = scatter_about(key_of[6], (REQUESTS, D), 1.0, 6.0, ((0, 32), (1, 4)))
    norm_gain = jnp.clip(1.0 + 0.18 * jax.random.normal(key_of[7], (D,), jnp.float32), 0.099609375, 1.8984375).astype(jnp.bfloat16)
    w_router = scatter_about(key_of[8], (D, EXPERTS), D ** -0.5, 0.078125, ((0, 4),))
    expert_ids_keys = jax.random.split(jax.random.fold_in(key_of[9], 1), REQUESTS // REQ_DEV)
    expert_ids_turns = jax.random.permutation(jax.random.fold_in(key_of[9], 3), REQUESTS // REQ_DEV)
    expert_ids = jax.vmap(lambda own, number: shared_out(jax.random.fold_in(key_of[9], 2), own, number, REQ_DEV, EXPERTS, TOP, CAP, 2))(expert_ids_keys, expert_ids_turns).reshape((REQUESTS, TOP))
    w_gate = scatter_about(key_of[10], (D, EXPERTS * FF_WIN), D ** -0.5, 0.078125, ((1, 128),))
    w_up = scatter_about(key_of[11], (D, EXPERTS * FF_WIN), D ** -0.5, 0.078125, ((1, 128),))
    w_down = scatter_about(key_of[12], (EXPERTS * FF_WIN, D), FF_WIN ** -0.5, 0.0625, ((0, 128),))
    return {"queries": queries, "key_cache": key_cache, "value_cache": value_cache, "key_new": key_new, "value_new": value_new, "lengths": lengths, "residual": residual, "norm_gain": norm_gain, "w_router": w_router, "expert_ids": expert_ids, "w_gate": w_gate, "w_up": w_up, "w_down": w_down}


def attend(queries, key_cache, value_cache, key_new, value_new, lengths):
    rows = queries.shape[0]
    heads_kv = key_new.shape[1] // HD
    repeat = queries.shape[1] // HD // heads_kv
    length = key_cache.shape[1]
    scale = 1.0 / HD ** 0.5
    qhead = queries.astype(jnp.float32).reshape(rows, heads_kv, repeat, HD)
    kcache = key_cache.astype(jnp.float32).reshape(rows, length, heads_kv, HD)
    vcache = value_cache.astype(jnp.float32).reshape(rows, length, heads_kv, HD)
    knew = key_new.astype(jnp.float32).reshape(rows, heads_kv, HD)
    vnew = value_new.astype(jnp.float32).reshape(rows, heads_kv, 1, HD)
    scores = jnp.einsum('rgho,rcgo->rghc', qhead, kcache) * scale
    own = jnp.einsum('rgho,rgo->rgh', qhead, knew) * scale
    valid = jnp.arange(length, dtype=jnp.int32)[None, :] < lengths[:, None]
    scores = jnp.where(valid[:, None, None, :], scores, -1e+30)
    top = jnp.maximum(lax.optimization_barrier(jnp.max(scores, -1)), own)
    probs = jnp.exp(scores - top[..., None])
    pown = jnp.exp(own - top)
    total = lax.optimization_barrier(jnp.sum(probs, -1)) + pown
    weights = (probs / total[..., None]).astype(jnp.bfloat16).astype(jnp.float32)
    wown = (pown / total).astype(jnp.bfloat16).astype(jnp.float32)
    result = jnp.einsum('rghc,rcgo->rgho', weights, vcache) + wown[..., None] * vnew
    return result.reshape(rows, repeat * heads_kv * HD)

def reference(queries, key_cache, value_cache, key_new, value_new, lengths, residual, norm_gain, w_router, expert_ids, w_gate, w_up, w_down):
    attn = attend(queries, key_cache, value_cache, key_new, value_new, lengths)
    hidden_state = (residual.astype(jnp.float32) + attn).astype(jnp.bfloat16)
    hfloat = hidden_state.astype(jnp.float32)
    meansq = lax.optimization_barrier(jnp.mean(hfloat * hfloat, -1, keepdims=True))
    normed = (hfloat * lax.rsqrt(meansq + 1e-05) * norm_gain.astype(jnp.float32)).astype(jnp.bfloat16)
    logits = jnp.dot(normed, w_router, preferred_element_type=jnp.float32)
    chosen = jnp.take_along_axis(logits, expert_ids, 1)
    gates = jax.nn.softmax(chosen, -1)
    onehot = (expert_ids[:, :, None] == jnp.arange(EXPERTS, dtype=jnp.int32)[None, None, :]).astype(jnp.float32)
    mixing = lax.optimization_barrier(jnp.sum(gates[:, :, None] * onehot, 1))

    def one_expert(carry, index):
        start = (index * FF_WIN).astype(jnp.int32)
        wgate = lax.dynamic_slice_in_dim(w_gate, start, FF_WIN, 1)
        wup = lax.dynamic_slice_in_dim(w_up, start, FF_WIN, 1)
        wdown = lax.dynamic_slice_in_dim(w_down, start, FF_WIN, 0)
        gate = jnp.dot(normed, wgate, preferred_element_type=jnp.float32)
        upper = jnp.dot(normed, wup, preferred_element_type=jnp.float32)
        act = (jax.nn.silu(gate) * upper).astype(jnp.bfloat16)
        outcome = jnp.dot(act, wdown, preferred_element_type=jnp.float32)
        column = lax.dynamic_slice_in_dim(mixing, index, 1, 1)
        return (carry + column * outcome, None)
    moe, _ = lax.scan(one_expert, jnp.zeros(hfloat.shape, jnp.float32), jnp.arange(EXPERTS, dtype=jnp.int32))
    return (hfloat + moe).astype(jnp.bfloat16)
```

```python
import functools

import jax
import jax.numpy as jnp
from jax import lax
from jax.experimental import pallas as pl
from jax.experimental.pallas import tpu as pltpu
from jax.sharding import Mesh
from jax.sharding import PartitionSpec as P

HD = 128
TOP = 2
CAP = 16
RING = 4
GROUPS = 1
bf16 = jnp.bfloat16
f32 = jnp.float32


def attend(queries, key_cache, value_cache, key_new, value_new, lengths):
    rows = queries.shape[0]
    heads_kv = key_new.shape[1] // HD
    repeat = queries.shape[1] // HD // heads_kv
    length = key_cache.shape[1]
    scale = 1.0 / HD**0.5
    qhead = queries.reshape(rows, heads_kv, repeat, HD)
    kcache = key_cache.reshape(rows, length, heads_kv, HD)
    vcache = value_cache.reshape(rows, length, heads_kv, HD)
    knew = key_new.reshape(rows, heads_kv, HD)
    vnew = value_new.reshape(rows, heads_kv, 1, HD).astype(f32)
    scores = jnp.einsum("rgho,rcgo->rghc", qhead, kcache, preferred_element_type=f32) * scale
    own = jnp.einsum("rgho,rgo->rgh", qhead, knew, preferred_element_type=f32) * scale
    valid = jnp.arange(length, dtype=jnp.int32)[None, :] < lengths[:, None]
    scores = jnp.where(valid[:, None, None, :], scores, -1e30)
    top = jnp.maximum(jnp.max(scores, -1), own)
    probs = jnp.exp(scores - top[..., None])
    pown = jnp.exp(own - top)
    total = jnp.sum(probs, -1) + pown
    weights = (probs / total[..., None]).astype(bf16)
    wown = (pown / total).astype(bf16).astype(f32)
    result = (
        jnp.einsum("rghc,rcgo->rgho", weights, vcache, preferred_element_type=f32)
        + wown[..., None] * vnew
    )
    return result.reshape(rows, repeat * heads_kv * HD)


def along(x, axis, by):
    return lax.ppermute(x, axis, [(i, (i + by) % RING) for i in range(RING)])


def swap_cores(x):
    return lax.ppermute(x, "pool", [(0, 1), (1, 0)])


def cross(x, leg, by):
    pairs = []
    for core in range(2):
        for i in range(RING):
            for j in range(RING):
                to = ((i + by) % RING, j) if core == leg else (i, (j + by) % RING)
                pairs.append((core * 16 + i * RING + j, core * 16 + to[0] * RING + to[1]))
    return lax.ppermute(x, ("pool", "x", "tp"), pairs)


def expert_kernel(
    place, own, above, below, far_a, far_b, inverse, w_gate, w_up, w_down,
    out_own, out_above, out_below, out_far_a, out_far_b,
    rows, gates, ups, downs, gate, upper, square, act, row_sem, gate_sem, up_sem, down_sem, out_sem,
):
    core, me = place[0], place[1]
    _, _, block, features = rows.shape
    units = gate.shape[1]
    count = RING * block

    def part(refs, outer, inner):
        first, second, far_1, far_2, third = refs
        if outer == 2:
            return far_1.at[inner] if inner < 2 else far_2.at[inner - 2]
        return {0: first, 1: second, 3: third}[outer].at[inner]

    def turned(quarter):
        return pl.ds(pl.multiple_of(lax.rem(me + quarter, RING) * features, features), features)

    arrived = (own, above, far_a, far_b, below)
    leaving = (out_own, out_above, out_far_a, out_far_b, out_below)

    def fetch(quarter, piece, flipped):
        source = part(arrived, piece, quarter) if flipped else part(arrived, quarter, piece)
        return pltpu.make_async_copy(source, rows.at[quarter, piece], row_sem.at[quarter, piece])

    def put(quarter, piece, flipped):
        target = part(leaving, piece, quarter) if flipped else part(leaving, quarter, piece)
        return pltpu.make_async_copy(rows.at[quarter, piece], target, out_sem.at[quarter, piece])

    def fetch_gate(quarter):
        return pltpu.make_async_copy(w_gate.at[turned(quarter), :], gates.at[quarter], gate_sem.at[quarter])

    def fetch_up(quarter):
        return pltpu.make_async_copy(w_up.at[turned(quarter), :], ups.at[quarter], up_sem.at[quarter])

    def fetch_down(quarter):
        return pltpu.make_async_copy(w_down.at[:, turned(quarter)], downs.at[quarter], down_sem.at[quarter])

    for quarter in range(RING):
        for flipped in range(2):
            @pl.when(core == flipped)
            def _():
                for piece in range(RING):
                    fetch(quarter, piece, flipped).start()
        fetch_gate(quarter).start()
        fetch_up(quarter).start()
    for quarter in range(RING):
        fetch_down(quarter).start()

    gate[...] = jnp.zeros_like(gate)
    upper[...] = jnp.zeros_like(upper)
    square[...] = jnp.zeros_like(square)

    @pl.loop(0, RING)
    def _(quarter):
        for piece in range(RING):
            pltpu.make_async_copy(
                own.at[0], rows.at[quarter, piece], row_sem.at[quarter, piece]
            ).wait()
        fetch_gate(quarter).wait()
        held = rows[quarter].reshape(count, features)
        gate[...] += jnp.dot(held, gates[quarter], preferred_element_type=f32)
        fetch_up(quarter).wait()
        upper[...] += jnp.dot(held, ups[quarter], preferred_element_type=f32)

        @pl.loop(0, features // 128)
        def _(lane):
            lanes = pl.ds(pl.multiple_of(lane * 128, 128), 128)
            plain = rows[quarter, :, :, lanes].reshape(count, 128).astype(f32) * inverse[quarter, :, lanes]
            square[...] += plain * plain

    mean = jnp.sum(square[...], -1, keepdims=True) / (RING * features)
    scale = lax.rsqrt(mean + 1e-05)
    scaled = gate[...] * scale
    act[...] = (scaled * jax.nn.sigmoid(scaled) * (upper[...] * scale)).astype(bf16)

    @pl.loop(0, RING)
    def _(quarter):
        fetch_down(quarter).wait()
        outcome = jnp.dot(act[...], downs[quarter], preferred_element_type=f32)
        rows[quarter] = outcome.astype(bf16).reshape(RING, block, features)
        for which in range(RING):
            for flipped in range(2):
                @pl.when((core == flipped) & (quarter == which))
                def _():
                    for piece in range(RING):
                        put(which, piece, flipped).start()

    for quarter in range(RING):
        for piece in range(RING):
            put(quarter, piece, 0).wait()


def expert(place, pieces, inverse, w_gate, w_up, w_down):
    own, above, below, far_a, far_b = pieces
    _, block, features = own.shape
    units = w_gate.shape[1]
    whole = jax.ShapeDtypeStruct(own.shape, bf16)
    half = jax.ShapeDtypeStruct(far_a.shape, bf16)
    anywhere = pl.BlockSpec(memory_space=pl.ANY)
    count = RING * block
    return pl.pallas_call(
        expert_kernel,
        out_shape=[whole, whole, whole, half, half],
        in_specs=[pl.BlockSpec(memory_space=pltpu.SMEM)]
        + [anywhere] * 5
        + [pl.BlockSpec(memory_space=pltpu.VMEM)]
        + [anywhere] * 3,
        out_specs=[anywhere] * 5,
        scratch_shapes=[
            pltpu.VMEM((RING, RING, block, features), bf16),
            pltpu.VMEM((RING, features, units), bf16),
            pltpu.VMEM((RING, features, units), bf16),
            pltpu.VMEM((RING, units, features), bf16),
            pltpu.VMEM((count, units), f32),
            pltpu.VMEM((count, units), f32),
            pltpu.VMEM((count, 128), f32),
            pltpu.VMEM((count, units), bf16),
            pltpu.SemaphoreType.DMA((RING, RING)),
            pltpu.SemaphoreType.DMA((RING,)),
            pltpu.SemaphoreType.DMA((RING,)),
            pltpu.SemaphoreType.DMA((RING,)),
            pltpu.SemaphoreType.DMA((RING, RING)),
        ],
        compiler_params=pltpu.CompilerParams(vmem_limit_bytes=52 * 1024 * 1024),
        cost_estimate=pl.CostEstimate(
            flops=6 * count * RING * features * units,
            bytes_accessed=6 * RING * features * (units + count // 3),
            transcendentals=count * units,
        ),
        name="expert",
    )(place, own, above, below, far_a, far_b, inverse, w_gate, w_up, w_down)


def shards(
    queries, key_cache, value_cache, key_new, value_new, lengths, residual,
    norm_gain, w_router, expert_ids, w_gate, w_up, w_down,
):
    rows, features = residual.shape
    experts = w_router.shape[1]
    me_pool, me_z, me_y = lax.axis_index("pool"), lax.axis_index("z"), lax.axis_index("tp")
    place = jnp.stack([me_pool, me_y]).astype(jnp.int32)
    gains = [norm_gain, along(norm_gain, "tp", -1), along(norm_gain, "tp", 2), along(norm_gain, "tp", 1)]
    inverse = 1.0 / jnp.stack(gains).astype(f32)[:, None, :]

    attn = attend(queries, key_cache, value_cache, key_new, value_new, lengths)
    hidden_state = (residual.astype(f32) + attn).astype(bf16)
    hfloat = hidden_state.astype(f32)
    raised = (hfloat * norm_gain.astype(f32)[None, :]).astype(bf16)

    near = ((expert_ids // RING + me_pool) % 2) * RING + (expert_ids % RING - me_z + RING) % RING
    flat = near.reshape(-1)
    expert_hot = (flat[:, None] == jnp.arange(experts, dtype=jnp.int32)[None, :]).astype(jnp.int32)
    earlier = jnp.cumsum(expert_hot, 0) - expert_hot
    slot = jnp.sum(earlier * expert_hot, 1)
    size = CAP // GROUPS
    position = (((slot // size) * experts + flat) * size + slot % size).reshape(rows, TOP)
    places = jnp.arange(experts * CAP, dtype=jnp.int32)
    hot = position[:, :, None] == places[None, None, :]
    dispatch = jnp.any(hot, 1).T.astype(bf16)
    bucket = jnp.dot(dispatch, raised, preferred_element_type=f32).astype(bf16)
    buckets = bucket.reshape(GROUPS, 2, RING, size, features)

    stats = jnp.concatenate(
        [
            jnp.dot(raised, w_router, preferred_element_type=f32),
            jnp.sum(hfloat * hfloat, -1, keepdims=True),
        ],
        1,
    )

    returned = []
    for group in range(GROUPS):
        partner = swap_cores(buckets[group, 1])
        pairs = jnp.stack([buckets[group, 0], partner], 1).reshape(RING, 2 * size, features)
        block = jnp.concatenate([pairs[0]] + [along(pairs[d], "z", d) for d in range(1, RING)])
        first = jnp.stack([block, cross(block, 0, -1), cross(block, 0, 2), cross(block, 0, 1)])
        if group == 0:
            stats, first = lax.optimization_barrier((stats, first))
            stats = lax.psum(stats, "tp")
        above = cross(first, 1, -1)
        below = cross(first, 1, 1)
        far_a = cross(above[:2], 1, -1)
        far_b = cross(below[2:], 1, 1)
        if group == 0:
            stats, inverse = lax.optimization_barrier((stats, inverse))
        own_out, above_out, below_out, far_a_out, far_b_out = expert(
            place, (first, above, below, far_a, far_b), inverse, w_gate, w_up, w_down
        )
        relay_a = cross(far_a_out, 1, 1)
        relay_b = cross(far_b_out, 1, -1)
        up = jnp.concatenate([(above_out[:2].astype(f32) + relay_a.astype(f32)).astype(bf16), above_out[2:]])
        down = jnp.concatenate([below_out[:2], (below_out[2:].astype(f32) + relay_b.astype(f32)).astype(bf16)])
        from_below = cross(up, 1, 1)
        from_above = cross(down, 1, -1)
        mine = own_out.astype(f32) + from_below.astype(f32) + from_above.astype(f32)
        sent = mine.astype(bf16)
        total = mine[0]
        for d in range(1, RING):
            total = total + cross(sent[d], 0, d).astype(f32)
        back = total.astype(bf16).reshape(RING, 2, size, features)
        home = jnp.stack([back[0]] + [along(back[d], "z", -d) for d in range(1, RING)])
        returned.append(jnp.stack([home[:, 0], swap_cores(home[:, 1])]))

    logits = stats[:, :experts] * lax.rsqrt(stats[:, experts:] / (features * RING) + 1e-05)
    chosen = jnp.take_along_axis(logits, expert_ids, 1)
    gates = jax.nn.softmax(chosen, -1)
    combine = jnp.sum(jnp.where(hot, gates[:, :, None], 0.0), 1)
    results = jnp.stack(returned).reshape(experts * CAP, features)
    mixed = jnp.dot(combine, results.astype(f32), precision=lax.Precision.HIGHEST)
    return (hfloat + mixed).astype(bf16)


def solution(mesh):
    split = Mesh(mesh.devices.reshape(2, RING, RING, RING), ("pool", "z", "x", "tp"))
    rows = ("pool", "z", "x")
    every = ("pool", "z", "x", "tp")
    placed = (
        P(rows, "tp"),
        P(rows, None, "tp"),
        P(rows, None, "tp"),
        P(rows, "tp"),
        P(rows, "tp"),
        P(rows),
        P(rows, "tp"),
        P("tp"),
        P("tp", None),
        P(rows, None),
        P(None, every),
        P(None, every),
        P(every, None),
    )
    return jax.shard_map(
        shards, mesh=split, in_specs=placed, out_specs=P(rows, "tp"), check_vma=False
    )
```

```python
import functools

import jax
import jax.numpy as jnp
from jax import lax
from jax.experimental import pallas as pl
from jax.experimental.pallas import tpu as pltpu
from jax.sharding import Mesh
from jax.sharding import PartitionSpec as P

HD = 128
TOP = 2
CAP = 16
RING = 4
GROUPS = 1
bf16 = jnp.bfloat16
f32 = jnp.float32


def attend(queries, key_cache, value_cache, key_new, value_new, lengths):
    rows = queries.shape[0]
    heads_kv = key_new.shape[1] // HD
    repeat = queries.shape[1] // HD // heads_kv
    length = key_cache.shape[1]
    scale = 1.0 / HD**0.5
    qhead = queries.reshape(rows, heads_kv, repeat, HD)
    kcache = key_cache.reshape(rows, length, heads_kv, HD)
    vcache = value_cache.reshape(rows, length, heads_kv, HD)
    knew = key_new.reshape(rows, heads_kv, HD)
    vnew = value_new.reshape(rows, heads_kv, 1, HD).astype(f32)
    scores = jnp.einsum("rgho,rcgo->rghc", qhead, kcache, preferred_element_type=f32) * scale
    own = jnp.einsum("rgho,rgo->rgh", qhead, knew, preferred_element_type=f32) * scale
    valid = jnp.arange(length, dtype=jnp.int32)[None, :] < lengths[:, None]
    scores = jnp.where(valid[:, None, None, :], scores, -1e30)
    top = jnp.maximum(jnp.max(scores, -1), own)
    probs = jnp.exp(scores - top[..., None])
    pown = jnp.exp(own - top)
    total = jnp.sum(probs, -1) + pown
    weights = (probs / total[..., None]).astype(bf16)
    wown = (pown / total).astype(bf16).astype(f32)
    result = (
        jnp.einsum("rghc,rcgo->rgho", weights, vcache, preferred_element_type=f32)
        + wown[..., None] * vnew
    )
    return result.reshape(rows, repeat * heads_kv * HD)


def along(x, axis, by):
    return lax.ppermute(x, axis, [(i, (i + by) % RING) for i in range(RING)])


def swap_cores(x):
    return lax.ppermute(x, "pool", [(0, 1), (1, 0)])


def cross(x, leg, by):
    pairs = []
    for core in range(2):
        for i in range(RING):
            for j in range(RING):
                to = ((i + by) % RING, j) if core == leg else (i, (j + by) % RING)
                pairs.append((core * 16 + i * RING + j, core * 16 + to[0] * RING + to[1]))
    return lax.ppermute(x, ("pool", "x", "tp"), pairs)


ORDER = (0, 1, 3, 2)


def turned(me, quarter, features):
    return pl.ds(pl.multiple_of(lax.rem(me + quarter, RING) * features, features), features)


def pieces_of(flipped, arrived):
    if flipped:
        rows = [p for p in range(RING) if ORDER[p] in arrived]
        return [(q, [(p, arrived[ORDER[p]][q // 2].at[q % 2]) for p in rows]) for q in range(RING)]
    quarters = [q for q in ORDER if q in arrived]
    return [(q, [(p, arrived[q][ORDER[p] // 2].at[ORDER[p] % 2]) for p in range(RING)]) for q in quarters]


def bring_kernel(place, w_gate, w_up, w_down, gate_in, up_in, down_in, sem):
    pairs = ((w_gate, gate_in), (w_up, up_in), (w_down, down_in))
    copies = [pltpu.make_async_copy(source, target, sem.at[i]) for i, (source, target) in enumerate(pairs)]
    for copy in copies:
        copy.start()
    for copy in copies:
        copy.wait()


def early_kernel(
    place, own_0, own_1, above_0, above_1, below_0, below_1, w_gate, w_up, gate, upper, rows, sem
):
    core, me = place[0], place[1]
    _, _, block, features = rows.shape
    arrived = {0: (own_0, own_1), 1: (above_0, above_1), 3: (below_0, below_1)}
    gate[...] = jnp.zeros_like(gate)
    upper[...] = jnp.zeros_like(upper)

    for flipped in range(2):
        @pl.when(core == flipped)
        def _():
            work = pieces_of(flipped, arrived)
            for quarter, blocks in work:
                for p, source in blocks:
                    pltpu.make_async_copy(source, rows.at[quarter, p], sem.at[quarter, p]).start()
            for quarter, blocks in work:
                number = len(blocks)
                for p, source in blocks:
                    pltpu.make_async_copy(source, rows.at[quarter, p], sem.at[quarter, p]).wait()
                some = pl.ds(0, number * block)
                held = rows[quarter, :number].reshape(number * block, features)
                cut = turned(me, quarter, features)
                gate[some, :] += jnp.dot(held, w_gate[cut, :], preferred_element_type=f32)
                upper[some, :] += jnp.dot(held, w_up[cut, :], preferred_element_type=f32)


def late_kernel(place, far_0, far_1, gate_in, up_in, w_gate, w_up, w_down, act, out_0, out_1, rows, gate, upper, sem):
    core, me = place[0], place[1]
    _, block, features = rows.shape
    count = RING * block
    halves, outs = (far_0, far_1), (out_0, out_1)
    last = pl.ds((RING - 1) * block, block)

    for flipped in range(2):
        @pl.when(core == flipped)
        def _():
            for p in range(RING):
                inner = p if flipped else ORDER[p]
                pltpu.make_async_copy(halves[inner // 2].at[inner % 2], rows.at[p], sem.at[p]).start()

    gate[...] = gate_in[...]
    upper[...] = up_in[...]
    for p in range(RING):
        pltpu.make_async_copy(far_0.at[0], rows.at[p], sem.at[p]).wait()

    @pl.when(core == 0)
    def _():
        held = rows[...].reshape(count, features)
        gate[...] += jnp.dot(held, w_gate[turned(me, 2, features), :], preferred_element_type=f32)
        upper[...] += jnp.dot(held, w_up[turned(me, 2, features), :], preferred_element_type=f32)

    @pl.when(core == 1)
    def _():
        @pl.loop(0, RING)
        def _(quarter):
            gate[last, :] += jnp.dot(rows[quarter], w_gate[turned(me, quarter, features), :], preferred_element_type=f32)
            upper[last, :] += jnp.dot(rows[quarter], w_up[turned(me, quarter, features), :], preferred_element_type=f32)

    held = gate[...]
    act[...] = (held * jax.nn.sigmoid(held) * upper[...]).astype(bf16)

    @pl.when(core == 0)
    def _():
        outcome = jnp.dot(act[...], w_down[:, turned(me, 2, features)], preferred_element_type=f32).astype(bf16)
        for p in range(RING):
            outs[ORDER[p] // 2][ORDER[p] % 2] = outcome[p * block : (p + 1) * block]

    @pl.when(core == 1)
    def _():
        for quarter in range(RING):
            outs[quarter // 2][quarter % 2] = jnp.dot(
                act[last, :], w_down[:, turned(me, quarter, features)], preferred_element_type=f32
            ).astype(bf16)


def rest_kernel(place, act, w_down, own_0, own_1, above_0, above_1, below_0, below_1, rows, sem):
    core, me = place[0], place[1]
    _, _, block, features = rows.shape
    halves = {0: (own_0, own_1), 1: (above_0, above_1), 3: (below_0, below_1)}

    def step(quarter, blocks):
        outcome = jnp.dot(
            act[: blocks * block, :], w_down[:, turned(me, quarter, features)], preferred_element_type=f32
        )
        rows[quarter, :blocks] = outcome.astype(bf16).reshape(blocks, block, features)
        for p in range(blocks):
            if blocks < RING:
                target = halves[ORDER[p]][quarter // 2].at[quarter % 2]
            else:
                target = halves[quarter][ORDER[p] // 2].at[ORDER[p] % 2]
            pltpu.make_async_copy(rows.at[quarter, p], target, sem.at[quarter, p]).start()

    for flipped in range(2):
        @pl.when(core == flipped)
        def _():
            quarters, blocks = (range(RING), RING - 1) if flipped else ((1, 3, 0), RING)
            for quarter in quarters:
                step(quarter, blocks)
            for quarter in quarters:
                for p in range(blocks):
                    pltpu.make_async_copy(rows.at[quarter, p], own_0.at[0], sem.at[quarter, p]).wait()


ANYWHERE = pl.BlockSpec(memory_space=pl.ANY)
SCALARS = pl.BlockSpec(memory_space=pltpu.SMEM)
INSIDE = pl.BlockSpec(memory_space=pltpu.VMEM)
MIB = 1024 * 1024


def cost(macs, moved, raised=0):
    return pl.CostEstimate(flops=2 * macs, bytes_accessed=moved, transcendentals=raised)


def bring(place, w_gate, w_up, w_down):
    weights = [pltpu.with_memory_space_constraint(w, pltpu.HBM) for w in (w_gate, w_up, w_down)]
    return pl.pallas_call(
        bring_kernel,
        out_shape=[pltpu.VMEM(w.shape, bf16) for w in weights],
        in_specs=[SCALARS] + [pl.BlockSpec(memory_space=pltpu.HBM)] * 3,
        out_specs=[INSIDE] * 3,
        scratch_shapes=[pltpu.SemaphoreType.DMA((3,))],
        compiler_params=pltpu.CompilerParams(vmem_limit_bytes=MIB),
        cost_estimate=cost(0, 3 * w_gate.size * 2),
        name="bring",
    )(place, *weights)


def early(place, pieces, w_gate, w_up):
    _, block, features = pieces[0].shape
    units = w_gate.shape[1]
    count = RING * block
    return pl.pallas_call(
        early_kernel,
        out_shape=[jax.ShapeDtypeStruct((count, units), f32)] * 2,
        in_specs=[SCALARS] + [ANYWHERE] * 6 + [INSIDE] * 2,
        out_specs=[INSIDE] * 2,
        scratch_shapes=[
            pltpu.VMEM((RING, RING, block, features), bf16),
            pltpu.SemaphoreType.DMA((RING, RING)),
        ],
        compiler_params=pltpu.CompilerParams(vmem_limit_bytes=16 * MIB),
        cost_estimate=cost(3 * count * features * units * 2, 3 * count * features * 2),
        name="early",
    )(place, *pieces, w_gate, w_up)


def late(place, far, gate, upper, w_gate, w_up, w_down):
    _, block, features = far[0].shape
    units = w_gate.shape[1]
    count = RING * block
    half = jax.ShapeDtypeStruct(far[0].shape, bf16)
    return pl.pallas_call(
        late_kernel,
        out_shape=[jax.ShapeDtypeStruct((count, units), bf16), half, half],
        in_specs=[SCALARS] + [ANYWHERE] * 2 + [INSIDE] * 5,
        out_specs=[INSIDE] * 3,
        scratch_shapes=[
            pltpu.VMEM((RING, block, features), bf16),
            pltpu.VMEM((count, units), f32),
            pltpu.VMEM((count, units), f32),
            pltpu.SemaphoreType.DMA((RING,)),
        ],
        compiler_params=pltpu.CompilerParams(vmem_limit_bytes=16 * MIB),
        cost_estimate=cost(count * features * units * 3, 2 * count * features * 2, count * units),
        name="late",
    )(place, *far, gate, upper, w_gate, w_up, w_down)


def rest(place, act, w_down, shape):
    _, block, features = shape
    return pl.pallas_call(
        rest_kernel,
        out_shape=[jax.ShapeDtypeStruct(shape, bf16)] * 6,
        in_specs=[SCALARS] + [INSIDE] * 2,
        out_specs=[ANYWHERE] * 6,
        scratch_shapes=[
            pltpu.VMEM((RING, RING, block, features), bf16),
            pltpu.SemaphoreType.DMA((RING, RING)),
        ],
        compiler_params=pltpu.CompilerParams(vmem_limit_bytes=16 * MIB),
        cost_estimate=cost(3 * act.size * features, 3 * RING * block * features * 2),
        name="rest",
    )(place, act, w_down)


def shards(
    queries, key_cache, value_cache, key_new, value_new, lengths, residual,
    norm_gain, w_router, expert_ids, w_gate, w_up, w_down,
):
    rows, features = residual.shape
    experts = w_router.shape[1]
    me_pool, me_z, me_y = lax.axis_index("pool"), lax.axis_index("z"), lax.axis_index("tp")
    place = jnp.stack([me_pool, me_y]).astype(jnp.int32)

    attn = attend(queries, key_cache, value_cache, key_new, value_new, lengths)
    hidden_state = (residual.astype(f32) + attn).astype(bf16)
    hfloat = hidden_state.astype(f32)
    raised = hfloat * norm_gain.astype(f32)[None, :]
    stats = jnp.concatenate(
        [
            jnp.dot(raised.astype(bf16), w_router, preferred_element_type=f32),
            jnp.sum(hfloat * hfloat, -1, keepdims=True),
        ],
        1,
    )
    stats = stats + along(stats, "tp", 1) + along(stats, "tp", 2) + along(stats, "tp", 3)
    scale = lax.rsqrt(stats[:, experts:] / (features * RING) + 1e-05)
    normed = (raised * scale).astype(bf16)

    near = ((expert_ids // RING + me_pool) % 2) * RING + (expert_ids % RING - me_z + RING) % RING
    flat = near.reshape(-1)
    expert_hot = (flat[:, None] == jnp.arange(experts, dtype=jnp.int32)[None, :]).astype(jnp.int32)
    earlier = jnp.cumsum(expert_hot, 0) - expert_hot
    slot = jnp.sum(earlier * expert_hot, 1)
    size = CAP // GROUPS
    position = (((slot // size) * experts + flat) * size + slot % size).reshape(rows, TOP)
    places = jnp.arange(experts * CAP, dtype=jnp.int32)
    hot = position[:, :, None] == places[None, None, :]
    dispatch = jnp.any(hot, 1).T.astype(bf16)
    bucket = jnp.dot(dispatch, normed, preferred_element_type=f32).astype(bf16)
    buckets = bucket.reshape(GROUPS, 2, RING, size, features)

    returned = []
    for group in range(GROUPS):
        partner = swap_cores(buckets[group, 1])
        pairs = jnp.stack([buckets[group, 0], partner], 1).reshape(RING, 2 * size, features)
        block = jnp.concatenate([pairs[0]] + [along(pairs[d], "z", d) for d in range(1, RING)])
        near_block, last_block = cross(block, 0, -1), cross(block, 0, 1)
        if group == 0:
            place, block = lax.optimization_barrier((place, block))
            weights = bring(place, w_gate, w_up, w_down)
            near_block, weights = lax.optimization_barrier((near_block, weights))
            gate_in, up_in, down_in = weights
        near_block, kept = lax.optimization_barrier((near_block, block))
        far_block = cross(kept, 0, 2)
        own = [jnp.stack([block, near_block]), jnp.stack([far_block, last_block])]
        above, below = [None, None], [None, None]
        for half in range(2):
            above[half] = cross(own[half], 1, -1)
            below[half] = cross(own[half], 1, 1)
        below = lax.optimization_barrier(below)
        far = [cross(above[0], 1, -1), cross(below[1], 1, 1)]
        gate, upper = early(place, own + above + below, gate_in, up_in)
        act, far_0, far_1 = late(place, far, gate, upper, gate_in, up_in, down_in)
        relay_0, relay_1 = cross(far_0, 1, 1), cross(far_1, 1, -1)
        own_0, own_1, above_0, above_1, below_0, below_1 = rest(place, act, down_in, far_0.shape)
        up_1 = cross(above_1, 1, 1)
        down_0 = cross(below_0, 1, -1)
        up_0 = cross((above_0.astype(f32) + relay_0.astype(f32)).astype(bf16), 1, 1)
        down_1 = cross((below_1.astype(f32) + relay_1.astype(f32)).astype(bf16), 1, -1)
        terms = ((own_0, up_0, down_0), (own_1, up_1, down_1))
        def mine(d):
            return sum(t[d % 2].astype(f32) for t in terms[d // 2])

        parts = [cross(mine(d).astype(bf16), 0, d) for d in (1, 2, 3)]
        terms, parts = lax.optimization_barrier((terms, parts))
        total = mine(0) + sum(p.astype(f32) for p in parts)
        back = total.astype(bf16).reshape(RING, 2, size, features)
        home = jnp.stack([back[0]] + [along(back[d], "z", -d) for d in range(1, RING)])
        returned.append(jnp.stack([home[:, 0], swap_cores(home[:, 1])]))

    logits = stats[:, :experts] * scale
    chosen = jnp.take_along_axis(logits, expert_ids, 1)
    gates = jax.nn.softmax(chosen, -1)
    combine = jnp.sum(jnp.where(hot, gates[:, :, None], 0.0), 1)
    results = jnp.stack(returned).reshape(experts * CAP, features)
    mixed = jnp.dot(combine, results.astype(f32), precision=lax.Precision.HIGHEST)
    return (hfloat + mixed).astype(bf16)


def solution(mesh):
    split = Mesh(mesh.devices.reshape(2, RING, RING, RING), ("pool", "z", "x", "tp"))
    rows = ("pool", "z", "x")
    every = ("pool", "z", "x", "tp")
    placed = (
        P(rows, "tp"),
        P(rows, None, "tp"),
        P(rows, None, "tp"),
        P(rows, "tp"),
        P(rows, "tp"),
        P(rows),
        P(rows, "tp"),
        P("tp"),
        P("tp", None),
        P(rows, None),
        P(None, every),
        P(None, every),
        P(every, None),
    )
    return jax.shard_map(
        shards, mesh=split, in_specs=placed, out_specs=P(rows, "tp"), check_vma=False
    )
```

```python
import functools

import jax
import jax.numpy as jnp
from jax import lax
from jax.experimental import pallas as pl
from jax.experimental.pallas import tpu as pltpu
from jax.sharding import Mesh
from jax.sharding import PartitionSpec as P

HD = 128
TOP = 2
CAP = 16
RING = 4
GROUPS = 1
bf16 = jnp.bfloat16
f32 = jnp.float32


def attend(queries, key_cache, value_cache, key_new, value_new, lengths):
    rows = queries.shape[0]
    heads_kv = key_new.shape[1] // HD
    repeat = queries.shape[1] // HD // heads_kv
    length = key_cache.shape[1]
    scale = 1.0 / HD**0.5
    qhead = queries.reshape(rows, heads_kv, repeat, HD)
    kcache = key_cache.reshape(rows, length, heads_kv, HD)
    vcache = value_cache.reshape(rows, length, heads_kv, HD)
    knew = key_new.reshape(rows, heads_kv, HD)
    vnew = value_new.reshape(rows, heads_kv, 1, HD).astype(f32)
    scores = jnp.einsum("rgho,rcgo->rghc", qhead, kcache, preferred_element_type=f32) * scale
    own = jnp.einsum("rgho,rgo->rgh", qhead, knew, preferred_element_type=f32) * scale
    valid = jnp.arange(length, dtype=jnp.int32)[None, :] < lengths[:, None]
    scores = jnp.where(valid[:, None, None, :], scores, -1e30)
    top = jnp.maximum(jnp.max(scores, -1), own)
    probs = jnp.exp(scores - top[..., None])
    pown = jnp.exp(own - top)
    total = jnp.sum(probs, -1) + pown
    weights = (probs / total[..., None]).astype(bf16)
    wown = (pown / total).astype(bf16).astype(f32)
    result = (
        jnp.einsum("rghc,rcgo->rgho", weights, vcache, preferred_element_type=f32)
        + wown[..., None] * vnew
    )
    return result.reshape(rows, repeat * heads_kv * HD)


def along(x, axis, by):
    return lax.ppermute(x, axis, [(i, (i + by) % RING) for i in range(RING)])


def swap_cores(x):
    return lax.ppermute(x, "pool", [(0, 1), (1, 0)])


def cross(x, leg, by):
    pairs = []
    for core in range(2):
        for i in range(RING):
            for j in range(RING):
                to = ((i + by) % RING, j) if core == leg else (i, (j + by) % RING)
                pairs.append((core * 16 + i * RING + j, core * 16 + to[0] * RING + to[1]))
    return lax.ppermute(x, ("pool", "x", "tp"), pairs)


ORDER = (0, 1, 3, 2)


def turned(me, quarter, features):
    return pl.ds(pl.multiple_of(lax.rem(me + quarter, RING) * features, features), features)


def pieces_of(flipped, arrived):
    if flipped:
        rows = [p for p in range(RING) if ORDER[p] in arrived]
        return [(q, [(p, arrived[ORDER[p]][q // 2].at[q % 2]) for p in rows]) for q in range(RING)]
    quarters = [q for q in ORDER if q in arrived]
    return [(q, [(p, arrived[q][ORDER[p] // 2].at[ORDER[p] % 2]) for p in range(RING)]) for q in quarters]


def add_squares(square, rows, position, inverse):
    block, features = rows.shape
    total = jnp.zeros((block, 128), f32)
    for lane in range(0, features, 128):
        plain = rows[:, lane : lane + 128].astype(f32) * inverse[:, lane : lane + 128]
        total = total + plain * plain
    square[position * block : (position + 1) * block, :] += total


def early_kernel(
    place, own_0, own_1, above_0, above_1, below_0, below_1, inverse, w_gate, w_up,
    gate, upper, square, gate_in, up_in, rows, sem, gate_sem, up_sem,
):
    core, me = place[0], place[1]
    _, _, block, features = rows.shape
    arrived = {0: (own_0, own_1), 1: (above_0, above_1), 3: (below_0, below_1)}
    gate[...] = jnp.zeros_like(gate)
    upper[...] = jnp.zeros_like(upper)
    square[...] = jnp.zeros_like(square)

    def weights(quarter):
        cut = turned(me, quarter, features)
        return (
            pltpu.make_async_copy(w_gate.at[cut, :], gate_in.at[cut, :], gate_sem.at[quarter]),
            pltpu.make_async_copy(w_up.at[cut, :], up_in.at[cut, :], up_sem.at[quarter]),
        )

    for flipped in range(2):
        @pl.when(core == flipped)
        def _():
            work = dict(pieces_of(flipped, arrived))
            order = list(work) + [q for q in range(RING) if q not in work]

            def begin(step):
                if step < RING:
                    quarter = order[step]
                    for p, source in work.get(quarter, ()):
                        pltpu.make_async_copy(source, rows.at[quarter, p], sem.at[quarter, p]).start()
                    for copy in weights(quarter):
                        copy.start()

            begin(0)
            begin(1)
            for step, quarter in enumerate(order):
                blocks = work.get(quarter, ())
                for p, source in blocks:
                    pltpu.make_async_copy(source, rows.at[quarter, p], sem.at[quarter, p]).wait()
                for copy in weights(quarter):
                    copy.wait()
                begin(step + 2)
                if not blocks:
                    continue
                number = len(blocks)
                some = pl.ds(0, number * block)
                held = rows[quarter, :number].reshape(number * block, features)
                cut = turned(me, quarter, features)
                gate[some, :] += jnp.dot(held, gate_in[cut, :], preferred_element_type=f32)
                upper[some, :] += jnp.dot(held, up_in[cut, :], preferred_element_type=f32)
                for p, _ in blocks:
                    add_squares(square, rows.at[quarter, p], p, inverse.at[quarter])


def late_kernel(
    place, far_0, far_1, inverse, gate_in, up_in, square_in, w_gate, w_up, w_down,
    act, out_0, out_1, rows, gate, upper, square, downs, sem, down_sem,
):
    core, me = place[0], place[1]
    _, block, features = rows.shape
    count = RING * block
    halves, outs = (far_0, far_1), (out_0, out_1)
    last = pl.ds((RING - 1) * block, block)

    def fetch(quarter):
        return pltpu.make_async_copy(w_down.at[:, turned(me, quarter, features)], downs.at[quarter], down_sem.at[quarter])

    for flipped in range(2):
        @pl.when(core == flipped)
        def _():
            for p in range(RING):
                inner = p if flipped else ORDER[p]
                pltpu.make_async_copy(halves[inner // 2].at[inner % 2], rows.at[p], sem.at[p]).start()
            for quarter in range(RING) if flipped else (2,):
                fetch(quarter).start()

    gate[...] = gate_in[...]
    upper[...] = up_in[...]
    square[...] = square_in[...]
    for p in range(RING):
        pltpu.make_async_copy(far_0.at[0], rows.at[p], sem.at[p]).wait()

    @pl.when(core == 0)
    def _():
        held = rows[...].reshape(count, features)
        gate[...] += jnp.dot(held, w_gate[turned(me, 2, features), :], preferred_element_type=f32)
        upper[...] += jnp.dot(held, w_up[turned(me, 2, features), :], preferred_element_type=f32)
        for p in range(RING):
            add_squares(square, rows.at[p], p, inverse.at[2])

    @pl.when(core == 1)
    def _():
        @pl.loop(0, RING)
        def _(quarter):
            gate[last, :] += jnp.dot(rows[quarter], w_gate[turned(me, quarter, features), :], preferred_element_type=f32)
            upper[last, :] += jnp.dot(rows[quarter], w_up[turned(me, quarter, features), :], preferred_element_type=f32)
            add_squares(square, rows.at[quarter], RING - 1, inverse.at[quarter])

    mean = jnp.sum(square[...], -1, keepdims=True) / (RING * features)
    scale = lax.rsqrt(mean + 1e-05)
    held = gate[...] * scale
    act[...] = (held * jax.nn.sigmoid(held) * (upper[...] * scale)).astype(bf16)

    @pl.when(core == 0)
    def _():
        fetch(2).wait()
        outcome = jnp.dot(act[...], downs[2], preferred_element_type=f32).astype(bf16)
        for p in range(RING):
            outs[ORDER[p] // 2][ORDER[p] % 2] = outcome[p * block : (p + 1) * block]

    @pl.when(core == 1)
    def _():
        for quarter in range(RING):
            fetch(quarter).wait()
            outs[quarter // 2][quarter % 2] = jnp.dot(
                act[last, :], downs[quarter], preferred_element_type=f32
            ).astype(bf16)


def rest_kernel(place, act, w_down, own_0, own_1, above_0, above_1, below_0, below_1, rows, downs, sem, down_sem):
    core, me = place[0], place[1]
    _, _, block, features = rows.shape
    halves = {0: (own_0, own_1), 1: (above_0, above_1), 3: (below_0, below_1)}

    def fetch(quarter):
        return pltpu.make_async_copy(w_down.at[:, turned(me, quarter, features)], downs.at[quarter], down_sem.at[quarter])

    def step(quarter, blocks):
        fetch(quarter).wait()
        outcome = jnp.dot(act[: blocks * block, :], downs[quarter], preferred_element_type=f32)
        rows[quarter, :blocks] = outcome.astype(bf16).reshape(blocks, block, features)
        for p in range(blocks):
            if blocks < RING:
                target = halves[ORDER[p]][quarter // 2].at[quarter % 2]
            else:
                target = halves[quarter][ORDER[p] // 2].at[ORDER[p] % 2]
            pltpu.make_async_copy(rows.at[quarter, p], target, sem.at[quarter, p]).start()

    for flipped in range(2):
        @pl.when(core == flipped)
        def _():
            quarters, blocks = (range(RING), RING - 1) if flipped else ((1, 3, 0), RING)
            for quarter in quarters:
                fetch(quarter).start()
            for quarter in quarters:
                step(quarter, blocks)
            for quarter in quarters:
                for p in range(blocks):
                    pltpu.make_async_copy(rows.at[quarter, p], own_0.at[0], sem.at[quarter, p]).wait()


ANYWHERE = pl.BlockSpec(memory_space=pl.ANY)
SCALARS = pl.BlockSpec(memory_space=pltpu.SMEM)
INSIDE = pl.BlockSpec(memory_space=pltpu.VMEM)
MIB = 1024 * 1024


def cost(macs, moved, raised=0):
    return pl.CostEstimate(flops=2 * macs, bytes_accessed=moved, transcendentals=raised)


def early(place, pieces, inverse, w_gate, w_up):
    _, block, features = pieces[0].shape
    units = w_gate.shape[1]
    count = RING * block
    weights = [pltpu.with_memory_space_constraint(w, pltpu.HBM) for w in (w_gate, w_up)]
    return pl.pallas_call(
        early_kernel,
        out_shape=[jax.ShapeDtypeStruct((count, n), f32) for n in (units, units, 128)]
        + [pltpu.VMEM(w.shape, bf16) for w in weights],
        in_specs=[SCALARS] + [ANYWHERE] * 6 + [INSIDE] + [pl.BlockSpec(memory_space=pltpu.HBM)] * 2,
        out_specs=[INSIDE] * 5,
        scratch_shapes=[
            pltpu.VMEM((RING, RING, block, features), bf16),
            pltpu.SemaphoreType.DMA((RING, RING)),
            pltpu.SemaphoreType.DMA((RING,)),
            pltpu.SemaphoreType.DMA((RING,)),
        ],
        compiler_params=pltpu.CompilerParams(vmem_limit_bytes=16 * MIB),
        cost_estimate=cost(3 * count * features * units * 2, 3 * count * features * 2 + 4 * w_gate.size),
        name="early",
    )(place, *pieces, inverse, *weights)


def late(place, far, inverse, gate, upper, square, w_gate, w_up, w_down):
    _, block, features = far[0].shape
    units = w_gate.shape[1]
    count = RING * block
    half = jax.ShapeDtypeStruct(far[0].shape, bf16)
    return pl.pallas_call(
        late_kernel,
        out_shape=[jax.ShapeDtypeStruct((count, units), bf16), half, half],
        in_specs=[SCALARS] + [ANYWHERE] * 2 + [INSIDE] * 6 + [pl.BlockSpec(memory_space=pltpu.HBM)],
        out_specs=[INSIDE] * 3,
        scratch_shapes=[
            pltpu.VMEM((RING, block, features), bf16),
            pltpu.VMEM((count, units), f32),
            pltpu.VMEM((count, units), f32),
            pltpu.VMEM((count, 128), f32),
            pltpu.VMEM((RING, units, features), bf16),
            pltpu.SemaphoreType.DMA((RING,)),
            pltpu.SemaphoreType.DMA((RING,)),
        ],
        compiler_params=pltpu.CompilerParams(vmem_limit_bytes=20 * MIB),
        cost_estimate=cost(count * features * units * 3, 2 * count * features * 2, count * units),
        name="late",
    )(
        place, *far, inverse, gate, upper, square, w_gate, w_up,
        pltpu.with_memory_space_constraint(w_down, pltpu.HBM),
    )


def rest(place, act, w_down, shape):
    _, block, features = shape
    units = act.shape[1]
    return pl.pallas_call(
        rest_kernel,
        out_shape=[jax.ShapeDtypeStruct(shape, bf16)] * 6,
        in_specs=[SCALARS, INSIDE, pl.BlockSpec(memory_space=pltpu.HBM)],
        out_specs=[ANYWHERE] * 6,
        scratch_shapes=[
            pltpu.VMEM((RING, RING, block, features), bf16),
            pltpu.VMEM((RING, units, features), bf16),
            pltpu.SemaphoreType.DMA((RING, RING)),
            pltpu.SemaphoreType.DMA((RING,)),
        ],
        compiler_params=pltpu.CompilerParams(vmem_limit_bytes=20 * MIB),
        cost_estimate=cost(3 * act.size * features, 3 * RING * block * features * 2 + 2 * w_down.size),
        name="rest",
    )(place, act, pltpu.with_memory_space_constraint(w_down, pltpu.HBM))


def shards(
    queries, key_cache, value_cache, key_new, value_new, lengths, residual,
    norm_gain, w_router, expert_ids, w_gate, w_up, w_down,
):
    rows, features = residual.shape
    experts = w_router.shape[1]
    me_pool, me_z, me_y = lax.axis_index("pool"), lax.axis_index("z"), lax.axis_index("tp")
    place = jnp.stack([me_pool, me_y]).astype(jnp.int32)

    attn = attend(queries, key_cache, value_cache, key_new, value_new, lengths)
    hidden_state = (residual.astype(f32) + attn).astype(bf16)
    hfloat = hidden_state.astype(f32)
    raised = (hfloat * norm_gain.astype(f32)[None, :]).astype(bf16)
    stats = jnp.concatenate(
        [
            jnp.dot(raised, w_router, preferred_element_type=f32),
            jnp.sum(hfloat * hfloat, -1, keepdims=True),
        ],
        1,
    )
    shared = jnp.concatenate([stats.reshape(-1), norm_gain.astype(f32)])

    near = ((expert_ids // RING + me_pool) % 2) * RING + (expert_ids % RING - me_z + RING) % RING
    flat = near.reshape(-1)
    expert_hot = (flat[:, None] == jnp.arange(experts, dtype=jnp.int32)[None, :]).astype(jnp.int32)
    earlier = jnp.cumsum(expert_hot, 0) - expert_hot
    slot = jnp.sum(earlier * expert_hot, 1)
    size = CAP // GROUPS
    position = (((slot // size) * experts + flat) * size + slot % size).reshape(rows, TOP)
    places = jnp.arange(experts * CAP, dtype=jnp.int32)
    hot = position[:, :, None] == places[None, None, :]
    dispatch = jnp.any(hot, 1).T.astype(bf16)
    bucket = jnp.dot(dispatch, raised, preferred_element_type=f32).astype(bf16)
    buckets = bucket.reshape(GROUPS, 2, RING, size, features)

    returned = []
    for group in range(GROUPS):
        partner = swap_cores(buckets[group, 1])
        pairs = jnp.stack([buckets[group, 0], partner], 1).reshape(RING, 2 * size, features)
        block = jnp.concatenate([pairs[0]] + [along(pairs[d], "z", d) for d in range(1, RING)])
        if group == 0:
            twin = lax.ppermute(shared, "tp", [(i, i ^ 1) for i in range(RING)])
            block, twin = lax.optimization_barrier((block, twin))
            couple = jnp.stack([shared, twin])
            block, couple = lax.optimization_barrier((block, couple))
            others = lax.ppermute(couple, "tp", [(i, i ^ 2) for i in range(RING)])
        near_block, last_block = cross(block, 0, -1), cross(block, 0, 1)
        far_block = cross(block, 0, 2)
        if group == 0:
            far_block, others = lax.optimization_barrier((far_block, others))
            everyone = jnp.concatenate([couple, others])
            stats = jnp.sum(everyone[:, : stats.size], 0).reshape(stats.shape)
            scale = lax.rsqrt(stats[:, experts:] / (features * RING) + 1e-05)
            turns = jnp.arange(RING, dtype=jnp.int32)
            pick = (me_y ^ turns)[None, :] == ((me_y + turns) % RING)[:, None]
            gains = jnp.sum(jnp.where(pick[:, :, None], everyone[None, :, stats.size :], 0.0), 1)
            inverse = 1.0 / gains[:, None, :]
        own = [jnp.stack([block, near_block]), jnp.stack([far_block, last_block])]
        above, below = [None, None], [None, None]
        for half in range(2):
            above[half] = cross(own[half], 1, -1)
            below[half] = cross(own[half], 1, 1)
        far = [cross(above[0], 1, -1), cross(below[1], 1, 1)]
        gate, upper, square, gate_in, up_in = early(place, own + above + below, inverse, w_gate, w_up)
        act, far_0, far_1 = late(place, far, inverse, gate, upper, square, gate_in, up_in, w_down)
        relay_0, relay_1 = cross(far_0, 1, 1), cross(far_1, 1, -1)
        own_0, own_1, above_0, above_1, below_0, below_1 = rest(place, act, w_down, far_0.shape)
        up_1 = cross(above_1, 1, 1)
        down_0 = cross(below_0, 1, -1)
        up_0 = cross((above_0.astype(f32) + relay_0.astype(f32)).astype(bf16), 1, 1)
        down_1 = cross((below_1.astype(f32) + relay_1.astype(f32)).astype(bf16), 1, -1)
        terms = ((own_0, up_0, down_0), (own_1, up_1, down_1))
        def mine(d):
            return sum(t[d % 2].astype(f32) for t in terms[d // 2])

        parts = [cross(mine(d).astype(bf16), 0, d) for d in (1, 2, 3)]
        terms, parts = lax.optimization_barrier((terms, parts))
        total = mine(0) + sum(p.astype(f32) for p in parts)
        back = total.astype(bf16).reshape(RING, 2, size, features)
        home = jnp.stack([back[0]] + [along(back[d], "z", -d) for d in range(1, RING)])
        returned.append(jnp.stack([home[:, 0], swap_cores(home[:, 1])]))

    logits = stats[:, :experts] * scale
    chosen = jnp.take_along_axis(logits, expert_ids, 1)
    gates = jax.nn.softmax(chosen, -1)
    combine = jnp.sum(jnp.where(hot, gates[:, :, None], 0.0), 1)
    results = jnp.stack(returned).reshape(experts * CAP, features)
    mixed = jnp.dot(combine, results.astype(f32), precision=lax.Precision.HIGHEST)
    return (hfloat + mixed).astype(bf16)


def solution(mesh):
    split = Mesh(mesh.devices.reshape(2, RING, RING, RING), ("pool", "z", "x", "tp"))
    rows = ("pool", "z", "x")
    every = ("pool", "z", "x", "tp")
    placed = (
        P(rows, "tp"),
        P(rows, None, "tp"),
        P(rows, None, "tp"),
        P(rows, "tp"),
        P(rows, "tp"),
        P(rows),
        P(rows, "tp"),
        P("tp"),
        P("tp", None),
        P(rows, None),
        P(None, every),
        P(None, every),
        P(every, None),
    )
    return jax.shard_map(
        shards, mesh=split, in_specs=placed, out_specs=P(rows, "tp"), check_vma=False
    )
```

```python
import functools

import jax
import jax.numpy as jnp
from jax import lax
from jax.experimental import pallas as pl
from jax.experimental.pallas import tpu as pltpu
from jax.sharding import Mesh
from jax.sharding import PartitionSpec as P

HD = 128
TOP = 2
CAP = 16
RING = 4
GROUPS = 1
bf16 = jnp.bfloat16
f32 = jnp.float32


def attend(queries, key_cache, value_cache, key_new, value_new, lengths):
    rows = queries.shape[0]
    heads_kv = key_new.shape[1] // HD
    repeat = queries.shape[1] // HD // heads_kv
    length = key_cache.shape[1]
    scale = 1.0 / HD**0.5
    qhead = queries.reshape(rows, heads_kv, repeat, HD)
    kcache = key_cache.reshape(rows, length, heads_kv, HD)
    vcache = value_cache.reshape(rows, length, heads_kv, HD)
    knew = key_new.reshape(rows, heads_kv, HD)
    vnew = value_new.reshape(rows, heads_kv, 1, HD).astype(f32)
    scores = jnp.einsum("rgho,rcgo->rghc", qhead, kcache, preferred_element_type=f32) * scale
    own = jnp.einsum("rgho,rgo->rgh", qhead, knew, preferred_element_type=f32) * scale
    valid = jnp.arange(length, dtype=jnp.int32)[None, :] < lengths[:, None]
    scores = jnp.where(valid[:, None, None, :], scores, -1e30)
    top = jnp.maximum(jnp.max(scores, -1), own)
    probs = jnp.exp(scores - top[..., None])
    pown = jnp.exp(own - top)
    total = jnp.sum(probs, -1) + pown
    weights = (probs / total[..., None]).astype(bf16)
    wown = (pown / total).astype(bf16).astype(f32)
    result = (
        jnp.einsum("rghc,rcgo->rgho", weights, vcache, preferred_element_type=f32)
        + wown[..., None] * vnew
    )
    return result.reshape(rows, repeat * heads_kv * HD)


def along(x, axis, by):
    return lax.ppermute(x, axis, [(i, (i + by) % RING) for i in range(RING)])


def swap_cores(x):
    return lax.ppermute(x, "pool", [(0, 1), (1, 0)])


def cross(x, leg, by):
    pairs = []
    for core in range(2):
        for i in range(RING):
            for j in range(RING):
                to = ((i + by) % RING, j) if core == leg else (i, (j + by) % RING)
                pairs.append((core * 16 + i * RING + j, core * 16 + to[0] * RING + to[1]))
    return lax.ppermute(x, ("pool", "x", "tp"), pairs)


ORDER = (0, 1, 3, 2)


def turned(me, quarter, features):
    return pl.ds(pl.multiple_of(lax.rem(me + quarter, RING) * features, features), features)


def pieces_of(flipped, arrived):
    if flipped:
        rows = [p for p in range(RING) if ORDER[p] in arrived]
        return [(q, [(p, arrived[ORDER[p]][q // 2].at[q % 2]) for p in rows]) for q in range(RING)]
    quarters = [q for q in ORDER if q in arrived]
    return [(q, [(p, arrived[q][ORDER[p] // 2].at[ORDER[p] % 2]) for p in range(RING)]) for q in quarters]


def add_squares(square, rows, position, inverse):
    block, features = rows.shape
    total = jnp.zeros((block, 128), f32)
    for lane in range(0, features, 128):
        plain = rows[:, lane : lane + 128].astype(f32) * inverse[:, lane : lane + 128]
        total = total + plain * plain
    square[position * block : (position + 1) * block, :] += total


def add_products(
    core, me, arrived, more, inverse, w_gate, w_up,
    gate, upper, square, gate_in, up_in, rows, sem, gate_sem, up_sem,
):
    _, _, block, features = rows.shape

    def weights(quarter):
        cut = turned(me, quarter, features)
        return (
            pltpu.make_async_copy(w_gate.at[cut, :], gate_in.at[cut, :], gate_sem.at[quarter]),
            pltpu.make_async_copy(w_up.at[cut, :], up_in.at[cut, :], up_sem.at[quarter]),
        )

    for flipped in range(2):
        @pl.when(core == flipped)
        def _():
            work = dict(pieces_of(flipped, arrived))
            order = list(work) + [q for q in more if q not in work]

            def begin(step):
                if step < len(order):
                    quarter = order[step]
                    for p, source in work.get(quarter, ()):
                        pltpu.make_async_copy(source, rows.at[quarter, p], sem.at[quarter, p]).start()
                    for copy in weights(quarter):
                        copy.start()

            begin(0)
            begin(1)
            for step, quarter in enumerate(order):
                blocks = work.get(quarter, ())
                for p, source in blocks:
                    pltpu.make_async_copy(source, rows.at[quarter, p], sem.at[quarter, p]).wait()
                for copy in weights(quarter):
                    copy.wait()
                begin(step + 2)
                if not blocks:
                    continue
                low, number = blocks[0][0], len(blocks)
                some = pl.ds(low * block, number * block)
                held = rows[quarter, low : low + number].reshape(number * block, features)
                cut = turned(me, quarter, features)
                gate[some, :] += jnp.dot(held, gate_in[cut, :], preferred_element_type=f32)
                upper[some, :] += jnp.dot(held, up_in[cut, :], preferred_element_type=f32)
                for p, _ in blocks:
                    add_squares(square, rows.at[quarter, p], p, inverse.at[quarter])


def first_kernel(place, own_0, own_1, inverse, w_gate, w_up, gate, upper, square, gate_in, up_in, *scratch):
    gate[...] = jnp.zeros_like(gate)
    upper[...] = jnp.zeros_like(upper)
    square[...] = jnp.zeros_like(square)
    add_products(
        place[0], place[1], {0: (own_0, own_1)}, (), inverse, w_gate, w_up,
        gate, upper, square, gate_in, up_in, *scratch,
    )


def early_kernel(
    place, above_0, above_1, below_0, below_1, gate_0, up_0, square_0, inverse, w_gate, w_up,
    gate, upper, square, gate_in, up_in, *scratch,
):
    gate[...] = gate_0[...]
    upper[...] = up_0[...]
    square[...] = square_0[...]
    add_products(
        place[0], place[1], {1: (above_0, above_1), 3: (below_0, below_1)}, (2,), inverse, w_gate, w_up,
        gate, upper, square, gate_in, up_in, *scratch,
    )


def late_kernel(
    place, far_0, far_1, inverse, gate_in, up_in, square_in, w_gate, w_up, w_down,
    act, out_0, out_1, gate, upper, square, downs, down_sem,
):
    core, me = place[0], place[1]
    _, block, features = far_0.shape
    halves, outs = (far_0, far_1), (out_0, out_1)
    last = pl.ds((RING - 1) * block, block)

    def fetch(quarter):
        return pltpu.make_async_copy(w_down.at[:, turned(me, quarter, features)], downs.at[quarter], down_sem.at[quarter])

    for flipped in range(2):
        @pl.when(core == flipped)
        def _():
            for quarter in range(RING) if flipped else (2,):
                fetch(quarter).start()

    square[...] = square_in[...]

    @pl.when(core == 0)
    def _():
        cut = turned(me, 2, features)
        for half in range(2):
            held = halves[half][...].reshape(2 * block, features)
            more_gate = jnp.dot(held, w_gate[cut, :], preferred_element_type=f32)
            more_up = jnp.dot(held, w_up[cut, :], preferred_element_type=f32)
            for i in range(2):
                p = ORDER.index(2 * half + i)
                some = pl.ds(p * block, block)
                gate[some, :] = gate_in[some, :] + more_gate[i * block : (i + 1) * block]
                upper[some, :] = up_in[some, :] + more_up[i * block : (i + 1) * block]
                add_squares(square, halves[half].at[i], p, inverse.at[2])

    @pl.when(core == 1)
    def _():
        gate[...] = gate_in[...]
        upper[...] = up_in[...]
        for quarter in range(RING):
            cut = turned(me, quarter, features)
            piece = halves[quarter // 2].at[quarter % 2]
            gate[last, :] += jnp.dot(piece[...], w_gate[cut, :], preferred_element_type=f32)
            upper[last, :] += jnp.dot(piece[...], w_up[cut, :], preferred_element_type=f32)
            add_squares(square, piece, RING - 1, inverse.at[quarter])

    mean = jnp.sum(square[...], -1, keepdims=True) / (RING * features)
    scale = lax.rsqrt(mean + 1e-05)
    held = gate[...] * scale
    act[...] = (held * jax.nn.sigmoid(held) * (upper[...] * scale)).astype(bf16)

    @pl.when(core == 0)
    def _():
        fetch(2).wait()
        outcome = jnp.dot(act[...], downs[2], preferred_element_type=f32).astype(bf16)
        for p in range(RING):
            outs[ORDER[p] // 2][ORDER[p] % 2] = outcome[p * block : (p + 1) * block]

    @pl.when(core == 1)
    def _():
        for quarter in range(RING):
            fetch(quarter).wait()
            outs[quarter // 2][quarter % 2] = jnp.dot(
                act[last, :], downs[quarter], preferred_element_type=f32
            ).astype(bf16)


def rest_kernel(place, act, w_down, own_0, own_1, above_0, above_1, below_0, below_1, rows, downs, sem, down_sem):
    core, me = place[0], place[1]
    _, _, block, features = rows.shape
    halves = {0: (own_0, own_1), 1: (above_0, above_1), 3: (below_0, below_1)}

    def fetch(quarter):
        return pltpu.make_async_copy(w_down.at[:, turned(me, quarter, features)], downs.at[quarter], down_sem.at[quarter])

    def step(quarter, blocks):
        fetch(quarter).wait()
        outcome = jnp.dot(act[: blocks * block, :], downs[quarter], preferred_element_type=f32)
        rows[quarter, :blocks] = outcome.astype(bf16).reshape(blocks, block, features)
        for p in range(blocks):
            if blocks < RING:
                target = halves[ORDER[p]][quarter // 2].at[quarter % 2]
            else:
                target = halves[quarter][ORDER[p] // 2].at[ORDER[p] % 2]
            pltpu.make_async_copy(rows.at[quarter, p], target, sem.at[quarter, p]).start()

    for flipped in range(2):
        @pl.when(core == flipped)
        def _():
            quarters, blocks = (range(RING), RING - 1) if flipped else ((1, 3, 0), RING)
            for quarter in quarters:
                fetch(quarter).start()
            for quarter in quarters:
                step(quarter, blocks)
            for quarter in quarters:
                for p in range(blocks):
                    pltpu.make_async_copy(rows.at[quarter, p], own_0.at[0], sem.at[quarter, p]).wait()


ANYWHERE = pl.BlockSpec(memory_space=pl.ANY)
SCALARS = pl.BlockSpec(memory_space=pltpu.SMEM)
INSIDE = pl.BlockSpec(memory_space=pltpu.VMEM)
MIB = 1024 * 1024


def cost(macs, moved, raised=0):
    return pl.CostEstimate(flops=2 * macs, bytes_accessed=moved, transcendentals=raised)


def weighed(kernel, name, keep, place, pieces, begun, inverse, w_gate, w_up):
    _, block, features = pieces[0].shape
    units = w_gate.shape[1]
    count = RING * block
    weights = [pltpu.with_memory_space_constraint(w, pltpu.HBM) for w in (w_gate, w_up)]
    inside = [pltpu.VMEM(w.shape, bf16) for w in weights]
    return pl.pallas_call(
        kernel,
        out_shape=[jax.ShapeDtypeStruct((count, n), f32) for n in (units, units, 128)] + (inside if keep else []),
        in_specs=[SCALARS] + [ANYWHERE] * len(pieces) + [INSIDE] * (len(begun) + 1)
        + [pl.BlockSpec(memory_space=pltpu.HBM)] * 2,
        out_specs=[INSIDE] * (5 if keep else 3),
        scratch_shapes=([] if keep else inside)
        + [
            pltpu.VMEM((RING, RING, block, features), bf16),
            pltpu.SemaphoreType.DMA((RING, RING)),
            pltpu.SemaphoreType.DMA((RING,)),
            pltpu.SemaphoreType.DMA((RING,)),
        ],
        compiler_params=pltpu.CompilerParams(vmem_limit_bytes=(16 if keep else 28) * MIB),
        cost_estimate=cost(
            len(pieces) // 2 * count * features * units * 2, len(pieces) * count * features + 4 * w_gate.size
        ),
        name=name,
    )(place, *pieces, *begun, inverse, *weights)


def late(place, far, inverse, gate, upper, square, w_gate, w_up, w_down):
    _, block, features = far[0].shape
    units = w_gate.shape[1]
    count = RING * block
    half = jax.ShapeDtypeStruct(far[0].shape, bf16)
    return pl.pallas_call(
        late_kernel,
        out_shape=[jax.ShapeDtypeStruct((count, units), bf16), half, half],
        in_specs=[SCALARS] + [INSIDE] * 8 + [pl.BlockSpec(memory_space=pltpu.HBM)],
        out_specs=[INSIDE] * 3,
        scratch_shapes=[
            pltpu.VMEM((count, units), f32),
            pltpu.VMEM((count, units), f32),
            pltpu.VMEM((count, 128), f32),
            pltpu.VMEM((RING, units, features), bf16),
            pltpu.SemaphoreType.DMA((RING,)),
        ],
        compiler_params=pltpu.CompilerParams(vmem_limit_bytes=20 * MIB),
        cost_estimate=cost(count * features * units * 3, 2 * count * features * 2, count * units),
        name="late",
    )(
        place, *far, inverse, gate, upper, square, w_gate, w_up,
        pltpu.with_memory_space_constraint(w_down, pltpu.HBM),
    )


def rest(place, act, w_down, shape):
    _, block, features = shape
    units = act.shape[1]
    return pl.pallas_call(
        rest_kernel,
        out_shape=[jax.ShapeDtypeStruct(shape, bf16)] * 6,
        in_specs=[SCALARS, INSIDE, pl.BlockSpec(memory_space=pltpu.HBM)],
        out_specs=[ANYWHERE] * 6,
        scratch_shapes=[
            pltpu.VMEM((RING, RING, block, features), bf16),
            pltpu.VMEM((RING, units, features), bf16),
            pltpu.SemaphoreType.DMA((RING, RING)),
            pltpu.SemaphoreType.DMA((RING,)),
        ],
        compiler_params=pltpu.CompilerParams(vmem_limit_bytes=20 * MIB),
        cost_estimate=cost(3 * act.size * features, 3 * RING * block * features * 2 + 2 * w_down.size),
        name="rest",
    )(place, act, pltpu.with_memory_space_constraint(w_down, pltpu.HBM))


def shards(
    queries, key_cache, value_cache, key_new, value_new, lengths, residual,
    norm_gain, w_router, expert_ids, w_gate, w_up, w_down,
):
    rows, features = residual.shape
    experts = w_router.shape[1]
    me_pool, me_z, me_y = lax.axis_index("pool"), lax.axis_index("z"), lax.axis_index("tp")
    place = jnp.stack([me_pool, me_y]).astype(jnp.int32)

    attn = attend(queries, key_cache, value_cache, key_new, value_new, lengths)
    hidden_state = (residual.astype(f32) + attn).astype(bf16)
    hfloat = hidden_state.astype(f32)
    raised = (hfloat * norm_gain.astype(f32)[None, :]).astype(bf16)
    stats = jnp.concatenate(
        [
            jnp.dot(raised, w_router, preferred_element_type=f32),
            jnp.sum(hfloat * hfloat, -1, keepdims=True),
        ],
        1,
    )
    shared = jnp.concatenate([stats.reshape(-1), norm_gain.astype(f32)])

    near = ((expert_ids // RING + me_pool) % 2) * RING + (expert_ids % RING - me_z + RING) % RING
    flat = near.reshape(-1)
    expert_hot = (flat[:, None] == jnp.arange(experts, dtype=jnp.int32)[None, :]).astype(jnp.int32)
    earlier = jnp.cumsum(expert_hot, 0) - expert_hot
    slot = jnp.sum(earlier * expert_hot, 1)
    size = CAP // GROUPS
    position = (((slot // size) * experts + flat) * size + slot % size).reshape(rows, TOP)
    places = jnp.arange(experts * CAP, dtype=jnp.int32)
    hot = position[:, :, None] == places[None, None, :]
    dispatch = jnp.any(hot, 1).T.astype(bf16)
    bucket = jnp.dot(dispatch, raised, preferred_element_type=f32).astype(bf16)
    buckets = bucket.reshape(GROUPS, 2, RING, size, features)

    returned = []
    for group in range(GROUPS):
        partner = swap_cores(buckets[group, 1])
        pairs = jnp.stack([buckets[group, 0], partner], 1).reshape(RING, 2 * size, features)
        block = jnp.concatenate([pairs[0]] + [along(pairs[d], "z", d) for d in range(1, RING)])
        if group == 0:
            twin = lax.ppermute(shared, "tp", [(i, i ^ 1) for i in range(RING)])
            block, twin = lax.optimization_barrier((block, twin))
            couple = jnp.stack([shared, twin])
            block, couple = lax.optimization_barrier((block, couple))
            others = lax.ppermute(couple, "tp", [(i, i ^ 2) for i in range(RING)])
        near_block, last_block = cross(block, 0, -1), cross(block, 0, 1)
        far_block = cross(block, 0, 2)
        if group == 0:
            far_block, others = lax.optimization_barrier((far_block, others))
            everyone = jnp.concatenate([couple, others])
            stats = jnp.sum(everyone[:, : stats.size], 0).reshape(stats.shape)
            scale = lax.rsqrt(stats[:, experts:] / (features * RING) + 1e-05)
            turns = jnp.arange(RING, dtype=jnp.int32)
            pick = (me_y ^ turns)[None, :] == ((me_y + turns) % RING)[:, None]
            gains = jnp.sum(jnp.where(pick[:, :, None], everyone[None, :, stats.size :], 0.0), 1)
            inverse = 1.0 / gains[:, None, :]
        own = [jnp.stack([block, near_block]), jnp.stack([far_block, last_block])]
        above, below = [None, None], [None, None]
        for half in range(2):
            above[half] = cross(own[half], 1, -1)
            below[half] = cross(own[half], 1, 1)
        begun = weighed(first_kernel, "first", False, place, own, [], inverse, w_gate, w_up)
        begun, above[1] = lax.optimization_barrier((begun, above[1]))
        far = [cross(above[0], 1, -1), cross(below[1], 1, 1)]
        gate, upper, square, gate_in, up_in = weighed(
            early_kernel, "early", True, place, above + below, begun, inverse, w_gate, w_up
        )
        act, far_0, far_1 = late(place, far, inverse, gate, upper, square, gate_in, up_in, w_down)
        relay_0, relay_1 = cross(far_0, 1, 1), cross(far_1, 1, -1)
        own_0, own_1, above_0, above_1, below_0, below_1 = rest(place, act, w_down, far_0.shape)
        up_1 = cross(above_1, 1, 1)
        down_0 = cross(below_0, 1, -1)
        up_0 = cross((above_0.astype(f32) + relay_0.astype(f32)).astype(bf16), 1, 1)
        down_1 = cross((below_1.astype(f32) + relay_1.astype(f32)).astype(bf16), 1, -1)
        terms = ((own_0, up_0, down_0), (own_1, up_1, down_1))
        def mine(d):
            return sum(t[d % 2].astype(f32) for t in terms[d // 2])

        parts = [cross(mine(d).astype(bf16), 0, d) for d in (1, 2, 3)]
        terms, parts = lax.optimization_barrier((terms, parts))
        total = mine(0) + sum(p.astype(f32) for p in parts)
        back = total.astype(bf16).reshape(RING, 2, size, features)
        home = jnp.stack([back[0]] + [along(back[d], "z", -d) for d in range(1, RING)])
        returned.append(jnp.stack([home[:, 0], swap_cores(home[:, 1])]))

    logits = stats[:, :experts] * scale
    chosen = jnp.take_along_axis(logits, expert_ids, 1)
    gates = jax.nn.softmax(chosen, -1)
    combine = jnp.sum(jnp.where(hot, gates[:, :, None], 0.0), 1)
    results = jnp.stack(returned).reshape(experts * CAP, features)
    mixed = jnp.dot(combine, results.astype(f32), precision=lax.Precision.HIGHEST)
    return (hfloat + mixed).astype(bf16)


def solution(mesh):
    split = Mesh(mesh.devices.reshape(2, RING, RING, RING), ("pool", "z", "x", "tp"))
    rows = ("pool", "z", "x")
    every = ("pool", "z", "x", "tp")
    placed = (
        P(rows, "tp"),
        P(rows, None, "tp"),
        P(rows, None, "tp"),
        P(rows, "tp"),
        P(rows, "tp"),
        P(rows),
        P(rows, "tp"),
        P("tp"),
        P("tp", None),
        P(rows, None),
        P(None, every),
        P(None, every),
        P(every, None),
    )
    return jax.shard_map(
        shards, mesh=split, in_specs=placed, out_specs=P(rows, "tp"), check_vma=False
    )
```

```python
import functools

import jax
import jax.numpy as jnp
from jax import lax
from jax.experimental import pallas as pl
from jax.experimental.pallas import tpu as pltpu
from jax.sharding import Mesh
from jax.sharding import PartitionSpec as P

HD = 128
TOP = 2
CAP = 16
RING = 4
GROUPS = 1
bf16 = jnp.bfloat16
f32 = jnp.float32


def attend(queries, key_cache, value_cache, key_new, value_new, lengths):
    rows = queries.shape[0]
    heads_kv = key_new.shape[1] // HD
    repeat = queries.shape[1] // HD // heads_kv
    length = key_cache.shape[1]
    scale = 1.0 / HD**0.5
    qhead = queries.reshape(rows, heads_kv, repeat, HD)
    kcache = key_cache.reshape(rows, length, heads_kv, HD)
    vcache = value_cache.reshape(rows, length, heads_kv, HD)
    knew = key_new.reshape(rows, heads_kv, HD)
    vnew = value_new.reshape(rows, heads_kv, 1, HD).astype(f32)
    scores = jnp.einsum("rgho,rcgo->rghc", qhead, kcache, preferred_element_type=f32) * scale
    own = jnp.einsum("rgho,rgo->rgh", qhead, knew, preferred_element_type=f32) * scale
    valid = jnp.arange(length, dtype=jnp.int32)[None, :] < lengths[:, None]
    scores = jnp.where(valid[:, None, None, :], scores, -1e30)
    top = jnp.maximum(jnp.max(scores, -1), own)
    probs = jnp.exp(scores - top[..., None])
    pown = jnp.exp(own - top)
    total = jnp.sum(probs, -1) + pown
    weights = (probs / total[..., None]).astype(bf16)
    wown = (pown / total).astype(bf16).astype(f32)
    result = (
        jnp.einsum("rghc,rcgo->rgho", weights, vcache, preferred_element_type=f32)
        + wown[..., None] * vnew
    )
    return result.reshape(rows, repeat * heads_kv * HD)


def along(x, axis, by):
    return lax.ppermute(x, axis, [(i, (i + by) % RING) for i in range(RING)])


def swap_cores(x):
    return lax.ppermute(x, "pool", [(0, 1), (1, 0)])


def cross(x, leg, by):
    pairs = []
    for core in range(2):
        for i in range(RING):
            for j in range(RING):
                to = ((i + by) % RING, j) if core == leg else (i, (j + by) % RING)
                pairs.append((core * 16 + i * RING + j, core * 16 + to[0] * RING + to[1]))
    return lax.ppermute(x, ("pool", "x", "tp"), pairs)


ORDER = (0, 1, 3, 2)


def turned(me, quarter, features):
    return pl.ds(pl.multiple_of(lax.rem(me + quarter, RING) * features, features), features)


def pieces_of(flipped, arrived):
    if flipped:
        rows = [p for p in range(RING) if ORDER[p] in arrived]
        return [(q, [(p, arrived[ORDER[p]][q // 2].at[q % 2]) for p in rows]) for q in range(RING)]
    quarters = [q for q in ORDER if q in arrived]
    return [(q, [(p, arrived[q][ORDER[p] // 2].at[ORDER[p] % 2]) for p in range(RING)]) for q in quarters]


def add_squares(square, rows, position, inverse):
    block, features = rows.shape
    total = jnp.zeros((block, 128), f32)
    for lane in range(0, features, 128):
        plain = rows[:, lane : lane + 128].astype(f32) * inverse[:, lane : lane + 128]
        total = total + plain * plain
    square[position * block : (position + 1) * block, :] += total


def add_products(
    core, me, arrived, more, inverse, w_gate, w_up,
    gate, upper, square, gate_in, up_in, rows, sem, gate_sem, up_sem,
):
    _, _, block, features = rows.shape

    def weights(quarter):
        cut = turned(me, quarter, features)
        return (
            pltpu.make_async_copy(w_gate.at[cut, :], gate_in.at[cut, :], gate_sem.at[quarter]),
            pltpu.make_async_copy(w_up.at[cut, :], up_in.at[cut, :], up_sem.at[quarter]),
        )

    for flipped in range(2):
        @pl.when(core == flipped)
        def _():
            work = dict(pieces_of(flipped, arrived))
            order = list(work) + [q for q in more if q not in work]

            def begin(step):
                if step < len(order):
                    quarter = order[step]
                    for p, source in work.get(quarter, ()):
                        pltpu.make_async_copy(source, rows.at[quarter, p], sem.at[quarter, p]).start()
                    for copy in weights(quarter):
                        copy.start()

            begin(0)
            begin(1)
            for step, quarter in enumerate(order):
                blocks = work.get(quarter, ())
                for p, source in blocks:
                    pltpu.make_async_copy(source, rows.at[quarter, p], sem.at[quarter, p]).wait()
                for copy in weights(quarter):
                    copy.wait()
                begin(step + 2)
                if not blocks:
                    continue
                low, number = blocks[0][0], len(blocks)
                some = pl.ds(low * block, number * block)
                held = rows[quarter, low : low + number].reshape(number * block, features)
                cut = turned(me, quarter, features)
                gate[some, :] += jnp.dot(held, gate_in[cut, :], preferred_element_type=f32)
                upper[some, :] += jnp.dot(held, up_in[cut, :], preferred_element_type=f32)
                for p, _ in blocks:
                    add_squares(square, rows.at[quarter, p], p, inverse.at[quarter])


def first_kernel(place, own_0, own_1, inverse, w_gate, w_up, gate, upper, square, gate_in, up_in, *scratch):
    gate[...] = jnp.zeros_like(gate)
    upper[...] = jnp.zeros_like(upper)
    square[...] = jnp.zeros_like(square)
    add_products(
        place[0], place[1], {0: (own_0, own_1)}, (), inverse, w_gate, w_up,
        gate, upper, square, gate_in, up_in, *scratch,
    )


def early_kernel(
    place, above_0, above_1, below_0, below_1, gate_0, up_0, square_0, inverse, w_gate, w_up,
    gate, upper, square, gate_in, up_in, *scratch,
):
    gate[...] = gate_0[...]
    upper[...] = up_0[...]
    square[...] = square_0[...]
    add_products(
        place[0], place[1], {1: (above_0, above_1), 3: (below_0, below_1)}, (2,), inverse, w_gate, w_up,
        gate, upper, square, gate_in, up_in, *scratch,
    )


def late_kernel(
    place, far_0, far_1, inverse, gate_in, up_in, square_in, w_gate, w_up, w_down,
    act, out_0, out_1, gate, upper, square, downs, down_sem,
):
    core, me = place[0], place[1]
    _, block, features = far_0.shape
    halves, outs = (far_0, far_1), (out_0, out_1)
    last = pl.ds((RING - 1) * block, block)

    def fetch(quarter):
        return pltpu.make_async_copy(w_down.at[:, turned(me, quarter, features)], downs.at[quarter], down_sem.at[quarter])

    for flipped in range(2):
        @pl.when(core == flipped)
        def _():
            for quarter in range(RING) if flipped else (2,):
                fetch(quarter).start()

    square[...] = square_in[...]

    @pl.when(core == 0)
    def _():
        cut = turned(me, 2, features)
        for half in range(2):
            held = halves[half][...].reshape(2 * block, features)
            more_gate = jnp.dot(held, w_gate[cut, :], preferred_element_type=f32)
            more_up = jnp.dot(held, w_up[cut, :], preferred_element_type=f32)
            for i in range(2):
                p = ORDER.index(2 * half + i)
                some = pl.ds(p * block, block)
                gate[some, :] = gate_in[some, :] + more_gate[i * block : (i + 1) * block]
                upper[some, :] = up_in[some, :] + more_up[i * block : (i + 1) * block]
                add_squares(square, halves[half].at[i], p, inverse.at[2])

    @pl.when(core == 1)
    def _():
        gate[...] = gate_in[...]
        upper[...] = up_in[...]
        for quarter in range(RING):
            cut = turned(me, quarter, features)
            piece = halves[quarter // 2].at[quarter % 2]
            gate[last, :] += jnp.dot(piece[...], w_gate[cut, :], preferred_element_type=f32)
            upper[last, :] += jnp.dot(piece[...], w_up[cut, :], preferred_element_type=f32)
            add_squares(square, piece, RING - 1, inverse.at[quarter])

    mean = jnp.sum(square[...], -1, keepdims=True) / (RING * features)
    scale = lax.rsqrt(mean + 1e-05)
    held = gate[...] * scale
    act[...] = (held * jax.nn.sigmoid(held) * (upper[...] * scale)).astype(bf16)

    @pl.when(core == 0)
    def _():
        fetch(2).wait()
        outcome = jnp.dot(act[...], downs[2], preferred_element_type=f32).astype(bf16)
        for p in range(RING):
            outs[ORDER[p] // 2][ORDER[p] % 2] = outcome[p * block : (p + 1) * block]

    @pl.when(core == 1)
    def _():
        for quarter in range(RING):
            fetch(quarter).wait()
            outs[quarter // 2][quarter % 2] = jnp.dot(
                act[last, :], downs[quarter], preferred_element_type=f32
            ).astype(bf16)


def rest_kernel(place, act, w_down, own_0, own_1, above_0, above_1, below_0, below_1, rows, downs, sem, down_sem):
    core, me = place[0], place[1]
    _, _, block, features = rows.shape
    halves = {0: (own_0, own_1), 1: (above_0, above_1), 3: (below_0, below_1)}

    def fetch(quarter):
        return pltpu.make_async_copy(w_down.at[:, turned(me, quarter, features)], downs.at[quarter], down_sem.at[quarter])

    def step(quarter, blocks):
        fetch(quarter).wait()
        outcome = jnp.dot(act[: blocks * block, :], downs[quarter], preferred_element_type=f32)
        rows[quarter, :blocks] = outcome.astype(bf16).reshape(blocks, block, features)
        for p in range(blocks):
            if blocks < RING:
                target = halves[ORDER[p]][quarter // 2].at[quarter % 2]
            else:
                target = halves[quarter][ORDER[p] // 2].at[ORDER[p] % 2]
            pltpu.make_async_copy(rows.at[quarter, p], target, sem.at[quarter, p]).start()

    for flipped in range(2):
        @pl.when(core == flipped)
        def _():
            quarters, blocks = (range(RING), RING - 1) if flipped else ((1, 3, 0), RING)
            for quarter in quarters:
                fetch(quarter).start()
            for quarter in quarters:
                step(quarter, blocks)
            for quarter in quarters:
                for p in range(blocks):
                    pltpu.make_async_copy(rows.at[quarter, p], own_0.at[0], sem.at[quarter, p]).wait()


ANYWHERE = pl.BlockSpec(memory_space=pl.ANY)
SCALARS = pl.BlockSpec(memory_space=pltpu.SMEM)
INSIDE = pl.BlockSpec(memory_space=pltpu.VMEM)
MIB = 1024 * 1024


def cost(macs, moved, raised=0):
    return pl.CostEstimate(flops=2 * macs, bytes_accessed=moved, transcendentals=raised)


def weighed(kernel, name, keep, place, pieces, begun, inverse, w_gate, w_up):
    _, block, features = pieces[0].shape
    units = w_gate.shape[1]
    count = RING * block
    weights = [pltpu.with_memory_space_constraint(w, pltpu.HBM) for w in (w_gate, w_up)]
    inside = [pltpu.VMEM(w.shape, bf16) for w in weights]
    return pl.pallas_call(
        kernel,
        out_shape=[jax.ShapeDtypeStruct((count, n), f32) for n in (units, units, 128)] + (inside if keep else []),
        in_specs=[SCALARS] + [ANYWHERE] * len(pieces) + [INSIDE] * (len(begun) + 1)
        + [pl.BlockSpec(memory_space=pltpu.HBM)] * 2,
        out_specs=[INSIDE] * (5 if keep else 3),
        scratch_shapes=([] if keep else inside)
        + [
            pltpu.VMEM((RING, RING, block, features), bf16),
            pltpu.SemaphoreType.DMA((RING, RING)),
            pltpu.SemaphoreType.DMA((RING,)),
            pltpu.SemaphoreType.DMA((RING,)),
        ],
        compiler_params=pltpu.CompilerParams(vmem_limit_bytes=(16 if keep else 28) * MIB),
        cost_estimate=cost(
            len(pieces) // 2 * count * features * units * 2, len(pieces) * count * features + 4 * w_gate.size
        ),
        name=name,
    )(place, *pieces, *begun, inverse, *weights)


def late(place, far, inverse, gate, upper, square, w_gate, w_up, w_down):
    _, block, features = far[0].shape
    units = w_gate.shape[1]
    count = RING * block
    half = jax.ShapeDtypeStruct(far[0].shape, bf16)
    return pl.pallas_call(
        late_kernel,
        out_shape=[jax.ShapeDtypeStruct((count, units), bf16), half, half],
        in_specs=[SCALARS] + [INSIDE] * 8 + [pl.BlockSpec(memory_space=pltpu.HBM)],
        out_specs=[INSIDE] * 3,
        scratch_shapes=[
            pltpu.VMEM((count, units), f32),
            pltpu.VMEM((count, units), f32),
            pltpu.VMEM((count, 128), f32),
            pltpu.VMEM((RING, units, features), bf16),
            pltpu.SemaphoreType.DMA((RING,)),
        ],
        compiler_params=pltpu.CompilerParams(vmem_limit_bytes=20 * MIB),
        cost_estimate=cost(count * features * units * 3, 2 * count * features * 2, count * units),
        name="late",
    )(
        place, *far, inverse, gate, upper, square, w_gate, w_up,
        pltpu.with_memory_space_constraint(w_down, pltpu.HBM),
    )


def rest(place, act, w_down, shape):
    _, block, features = shape
    units = act.shape[1]
    return pl.pallas_call(
        rest_kernel,
        out_shape=[jax.ShapeDtypeStruct(shape, bf16)] * 6,
        in_specs=[SCALARS, INSIDE, pl.BlockSpec(memory_space=pltpu.HBM)],
        out_specs=[ANYWHERE] * 6,
        scratch_shapes=[
            pltpu.VMEM((RING, RING, block, features), bf16),
            pltpu.VMEM((RING, units, features), bf16),
            pltpu.SemaphoreType.DMA((RING, RING)),
            pltpu.SemaphoreType.DMA((RING,)),
        ],
        compiler_params=pltpu.CompilerParams(vmem_limit_bytes=20 * MIB),
        cost_estimate=cost(3 * act.size * features, 3 * RING * block * features * 2 + 2 * w_down.size),
        name="rest",
    )(place, act, pltpu.with_memory_space_constraint(w_down, pltpu.HBM))


def shards(
    queries, key_cache, value_cache, key_new, value_new, lengths, residual,
    norm_gain, w_router, expert_ids, w_gate, w_up, w_down,
):
    rows, features = residual.shape
    experts = w_router.shape[1]
    me_pool, me_z, me_y = lax.axis_index("pool"), lax.axis_index("z"), lax.axis_index("tp")
    place = jnp.stack([me_pool, me_y]).astype(jnp.int32)

    attn = attend(queries, key_cache, value_cache, key_new, value_new, lengths)
    hidden_state = (residual.astype(f32) + attn).astype(bf16)
    hfloat = hidden_state.astype(f32)
    raised = (hfloat * norm_gain.astype(f32)[None, :]).astype(bf16)
    stats = jnp.concatenate(
        [
            jnp.dot(raised, w_router, preferred_element_type=f32),
            jnp.sum(hfloat * hfloat, -1, keepdims=True),
        ],
        1,
    )
    shared = jnp.concatenate([stats.reshape(-1), norm_gain.astype(f32)])

    near = ((expert_ids // RING + me_pool) % 2) * RING + (expert_ids % RING - me_z + RING) % RING
    size = CAP // GROUPS
    wanted = near.T[:, None, :] == jnp.arange(experts, dtype=jnp.int32)[None, :, None]
    named = wanted[0] | wanted[1]
    tokens = jnp.arange(rows, dtype=jnp.int32)
    before = (tokens[:, None] < tokens[None, :]).astype(bf16)
    slot = jnp.dot(named.astype(bf16), before, preferred_element_type=f32)
    slots = jnp.arange(CAP, dtype=jnp.int32).astype(f32)
    hot = (slot[:, None, :] == slots[None, :, None]) & named[:, None, :]
    dispatch = hot.astype(bf16).reshape(experts * CAP, rows)
    bucket = jnp.dot(dispatch, raised, preferred_element_type=f32).astype(bf16)
    buckets = bucket.reshape(GROUPS, 2, RING, size, features)

    returned = []
    for group in range(GROUPS):
        partner = swap_cores(buckets[group, 1])
        pairs = jnp.stack([buckets[group, 0], partner], 1).reshape(RING, 2 * size, features)
        block = jnp.concatenate([pairs[0]] + [along(pairs[d], "z", d) for d in range(1, RING)])
        if group == 0:
            twin = lax.ppermute(shared, "tp", [(i, i ^ 1) for i in range(RING)])
            block, twin = lax.optimization_barrier((block, twin))
            couple = jnp.stack([shared, twin])
            block, couple = lax.optimization_barrier((block, couple))
            others = lax.ppermute(couple, "tp", [(i, i ^ 2) for i in range(RING)])
        near_block, last_block = cross(block, 0, -1), cross(block, 0, 1)
        far_block = cross(block, 0, 2)
        if group == 0:
            far_block, others = lax.optimization_barrier((far_block, others))
            everyone = jnp.concatenate([couple, others])
            stats = jnp.sum(everyone[:, : stats.size], 0).reshape(stats.shape)
            scale = lax.rsqrt(stats[:, experts:] / (features * RING) + 1e-05)
            turns = jnp.arange(RING, dtype=jnp.int32)
            pick = (me_y ^ turns)[None, :] == ((me_y + turns) % RING)[:, None]
            gains = jnp.sum(jnp.where(pick[:, :, None], everyone[None, :, stats.size :], 0.0), 1)
            inverse = 1.0 / gains[:, None, :]
        own = [jnp.stack([block, near_block]), jnp.stack([far_block, last_block])]
        above, below = [None, None], [None, None]
        for half in range(2):
            above[half] = cross(own[half], 1, -1)
            below[half] = cross(own[half], 1, 1)
        begun = weighed(first_kernel, "first", False, place, own, [], inverse, w_gate, w_up)
        begun, above[1] = lax.optimization_barrier((begun, above[1]))
        far = [cross(above[0], 1, -1), cross(below[1], 1, 1)]
        gate, upper, square, gate_in, up_in = weighed(
            early_kernel, "early", True, place, above + below, begun, inverse, w_gate, w_up
        )
        act, far_0, far_1 = late(place, far, inverse, gate, upper, square, gate_in, up_in, w_down)
        relay_0, relay_1 = cross(far_0, 1, 1), cross(far_1, 1, -1)
        own_0, own_1, above_0, above_1, below_0, below_1 = rest(place, act, w_down, far_0.shape)
        up_1 = cross(above_1, 1, 1)
        down_0 = cross(below_0, 1, -1)
        up_0 = cross((above_0.astype(f32) + relay_0.astype(f32)).astype(bf16), 1, 1)
        down_1 = cross((below_1.astype(f32) + relay_1.astype(f32)).astype(bf16), 1, -1)
        terms = ((own_0, up_0, down_0), (own_1, up_1, down_1))
        def mine(d):
            return sum(t[d % 2].astype(f32) for t in terms[d // 2])

        parts = [cross(mine(d).astype(bf16), 0, d) for d in (1, 2, 3)]
        terms, parts = lax.optimization_barrier((terms, parts))
        total = mine(0) + sum(p.astype(f32) for p in parts)
        back = total.astype(bf16).reshape(RING, 2, size, features)
        home = jnp.stack([back[0]] + [along(back[d], "z", -d) for d in range(1, RING)])
        returned.append(jnp.stack([home[:, 0], swap_cores(home[:, 1])]))

    logits = stats[:, :experts] * scale
    chosen = jnp.take_along_axis(logits, expert_ids, 1)
    gates = jax.nn.softmax(chosen, -1)
    share = jnp.sum(jnp.where(wanted, gates.T[:, None, :], 0.0), 0)
    combine = jnp.where(hot, share[:, None, :], 0.0).reshape(experts * CAP, rows).T
    results = jnp.stack(returned).reshape(experts * CAP, features)
    mixed = jnp.dot(combine, results.astype(f32), precision=lax.Precision.HIGHEST)
    return (hfloat + mixed).astype(bf16)


def solution(mesh):
    split = Mesh(mesh.devices.reshape(2, RING, RING, RING), ("pool", "z", "x", "tp"))
    rows = ("pool", "z", "x")
    every = ("pool", "z", "x", "tp")
    placed = (
        P(rows, "tp"),
        P(rows, None, "tp"),
        P(rows, None, "tp"),
        P(rows, "tp"),
        P(rows, "tp"),
        P(rows),
        P(rows, "tp"),
        P("tp"),
        P("tp", None),
        P(rows, None),
        P(None, every),
        P(None, every),
        P(every, None),
    )
    return jax.shard_map(
        shards, mesh=split, in_specs=placed, out_specs=P(rows, "tp"), check_vma=False
    )
```
